512 devices in a mesh: clip: 4 (over y), video: 32 (over z, core), audio: 4 (over x).
Axes of the slice: x: 4, y: 4, z: 16, core: 2. Of those that a mesh axis runs over, the one named last changes fastest.
Arguments:
- video_query: bfloat16 [16384, 3072], P(('clip', 'video'), 'audio'), parts along dimension 0, may hold values from -5 to 5
- video_key: bfloat16 [16384, 3072], P(('clip', 'video'), 'audio'), parts along dimension 0, may hold values from -5 to 5
- video_value: bfloat16 [16384, 3072], P(('clip', 'video'), 'audio'), parts along dimension 0, may hold values from -5 to 5
- video_cot: bfloat16 [16384, 3072], P(('clip', 'video'), 'audio'), parts along dimension 0, may hold values from -5 to 5
- audio_query: bfloat16 [8192, 3072], P(('clip', 'video'), 'audio'), parts along dimension 0, may hold values from -5 to 5
- audio_key: bfloat16 [8192, 3072], P(('clip', 'video'), 'audio'), parts along dimension 0, may hold values from -5 to 5
- audio_value: bfloat16 [8192, 3072], P(('clip', 'video'), 'audio'), parts along dimension 0, may hold values from -5 to 5
- audio_cot: bfloat16 [8192, 3072], P(('clip', 'video'), 'audio'), parts along dimension 0, may hold values from -5 to 5
- intersection: int32 [128, 2], P('clip'), parts along dimension 0, may hold values from 0 to 2048, as said below
Outputs:
- video_out: bfloat16 [16384, 3072], P(('clip', 'video'), 'audio'), parts along dimension 0
- audio_out: bfloat16 [8192, 3072], P(('clip', 'video'), 'audio'), parts along dimension 0
- video_query_grad: bfloat16 [16384, 3072], P(('clip', 'video'), 'audio'), parts along dimension 0
- video_key_grad: bfloat16 [16384, 3072], P(('clip', 'video'), 'audio'), parts along dimension 0
- video_value_grad: bfloat16 [16384, 3072], P(('clip', 'video'), 'audio'), parts along dimension 0
- audio_query_grad: bfloat16 [8192, 3072], P(('clip', 'video'), 'audio'), parts along dimension 0
- audio_key_grad: bfloat16 [8192, 3072], P(('clip', 'video'), 'audio'), parts along dimension 0
- audio_value_grad: bfloat16 [8192, 3072], P(('clip', 'video'), 'audio'), parts along dimension 0
The draws below stay inside these ranges and needn't reach their ends.
There are 4 independent parts, one for each index of `clip`. The reference program is written for one: setup_inputs(seed, part) draws one part's arguments, and reference() takes and returns one part's arrays. A program takes and returns all parts, laid end to end along the dimension named above; each array names one. Nothing has to cross between parts.
Inputs may be any that keep to these rules, and one draw needn't show every extreme that they name: `intersection`: row b holds two audio row numbers: the first lies from max(0, (b - 1) * 64) to b * 64, the second from (b + 1) * 64 to min(2048, (b + 2) * 64).
All inputs are finite; a program needn't handle non-finite values.
Results may differ from the reference program's by a relative error of at most 0.011.
Values may be sent and summed in bfloat16 or wider, within the bound.
A program may use at most 64 MiB of HBM per device.

```python
import jax
import jax.numpy as jnp
from jax import lax

H = 24
DH = 128
VTOK_DEV = 128
ATOK_DEV = 64
BLOCKS = 32
VTOK = 4096
ATOK = 2048


def drawn_rows(key, count):
    return jnp.clip(jax.random.normal(key, (count, H * DH), jnp.float32), -4.0, 4.0)


def draw_video_query(key, part):
    key = jax.random.fold_in(key, 11)
    return drawn_rows(key, BLOCKS * VTOK_DEV).astype(jnp.bfloat16)


def draw_audio_key(key, part):
    key = jax.random.fold_in(key, 12)
    return drawn_rows(key, BLOCKS * ATOK_DEV).astype(jnp.bfloat16)


def draw_audio_query(key, part):
    key = jax.random.fold_in(key, 13)
    return drawn_rows(key, BLOCKS * ATOK_DEV).astype(jnp.bfloat16)


def draw_video_key(key, part):
    key = jax.random.fold_in(key, 14)
    return drawn_rows(key, BLOCKS * VTOK_DEV).astype(jnp.bfloat16)


def draw_intersection(key, part):
    key = jax.random.fold_in(key, 15)
    lower_key, upper_key = jax.random.split(key)
    lower_reach = jax.random.randint(lower_key, (BLOCKS,), 0, ATOK_DEV + 1)
    upper_reach = jax.random.randint(upper_key, (BLOCKS,), 0, ATOK_DEV + 1)
    blocks = jnp.arange(BLOCKS, dtype=jnp.int32)
    firsts = jnp.maximum(blocks * ATOK_DEV - lower_reach, 0)
    lasts = jnp.minimum((blocks + 1) * ATOK_DEV + upper_reach, BLOCKS * ATOK_DEV)
    return jnp.stack([firsts, lasts], 1).astype(jnp.int32)


def block_levels(stream_key, extent, cuts, low, largest):
    level = 1.0
    for dim, blocks in cuts:
        steps = jax.random.uniform(jax.random.fold_in(jax.random.fold_in(stream_key, 6), dim), (blocks,), jnp.float32, low / len(cuts), largest / len(cuts))
        level = level * jnp.repeat(jnp.exp(steps), extent[dim] // blocks).reshape((-1,) + (1,) * (len(extent) - 1 - dim))
    return level


def scatter_about(rng, shape, scale, reach, cuts=(), kind=jnp.bfloat16):
    entries = jax.random.normal(rng, shape, jnp.float32) * scale
    if len(cuts) > 0:
        entries = block_levels(rng, shape, cuts, -0.22, 0.18) * entries
    return jnp.clip(entries, min=-reach, max=reach).astype(kind)


def setup_inputs(seed: int = 0, part: int = 0) -> dict:
    seeds = jax.random.split(jax.random.key(seed), 10)
    own_keys = jax.random.split(jax.random.fold_in(seeds[9], part), 10)
    video_query = draw_video_query(jax.random.fold_in(jax.random.fold_in(seeds[9], part), 71), part)
    video_key = draw_video_key(jax.random.fold_in(jax.random.fold_in(seeds[9], part), 71), part)
    video_value = scatter_about(own_keys[2], (VTOK, H * DH), 1.0, 5.0, ((0, 32), (1, 4)))
    video_cot = scatter_about(own_keys[3], (VTOK, H * DH), 1.0, 5.0, ((0, 32), (1, 4)))
    audio_query = draw_audio_query(jax.random.fold_in(jax.random.fold_in(seeds[9], part), 71), part)
    audio_key = draw_audio_key(jax.random.fold_in(jax.random.fold_in(seeds[9], part), 71), part)
    audio_value = scatter_about(own_keys[6], (ATOK, H * DH), 1.0, 5.0, ((0, 32), (1, 4)))
    audio_cot = scatter_about(own_keys[7], (ATOK, H * DH), 1.0, 5.0, ((0, 32), (1, 4)))
    intersection = draw_intersection(jax.random.fold_in(jax.random.fold_in(seeds[9], part), 71), part)
    return {"video_query": video_query, "video_key": video_key, "video_value": video_value, "video_cot": video_cot, "audio_query": audio_query, "audio_key": audio_key, "audio_value": audio_value, "audio_cot": audio_cot, "intersection": intersection}


NEG_FILL = -1.0e30
BEYOND = 1 << 30


def attend(queries, key_matrix, value_matrix, cotangent, present, score_scale):
    head_queries = queries.astype(jnp.float32).reshape(queries.shape[0], H, DH)
    head_keys = key_matrix.astype(jnp.float32).reshape(key_matrix.shape[0], H, DH)
    head_values = value_matrix.astype(jnp.float32).reshape(value_matrix.shape[0], H, DH)
    head_cotangents = cotangent.astype(jnp.float32).reshape(cotangent.shape[0], H, DH)
    scores = jnp.einsum("qhd,khd->hqk", head_queries, head_keys) * score_scale
    scores = jnp.where(present[None], scores, NEG_FILL)
    highest = jnp.max(scores, axis=2, keepdims=True)
    exponent = jnp.where(present[None], jnp.exp(scores - highest), 0.0)
    probability = exponent / jnp.sum(exponent, axis=2, keepdims=True)
    weights = lax.optimization_barrier(probability.astype(jnp.bfloat16)).astype(jnp.float32)
    unrounded = jnp.einsum("hqk,khd->qhd", weights, head_values)
    row_delta = jnp.sum(head_cotangents * unrounded, axis=2)
    prob_grad = jnp.einsum("qhd,khd->hqk", head_cotangents, head_values)
    score_grad = probability * (prob_grad - jnp.transpose(row_delta)[:, :, None])
    score_grad = lax.optimization_barrier(score_grad.astype(jnp.bfloat16)).astype(jnp.float32)
    query_grad = jnp.einsum("hqk,khd->qhd", score_grad, head_keys) * score_scale
    key_grad = jnp.einsum("hqk,qhd->khd", score_grad, head_queries) * score_scale
    value_grad = jnp.einsum("hqk,qhd->khd", weights, head_cotangents)
    width = H * DH
    return (unrounded.reshape(-1, width), query_grad.reshape(-1, width),
            key_grad.reshape(-1, width), value_grad.reshape(-1, width))


def window(matrix, block_index, rows):
    padded = jnp.pad(matrix, ((rows, rows), (0, 0)))
    return lax.dynamic_slice_in_dim(padded, block_index * rows, 3 * rows, 0)


def fold_windows(stacked, rows):
    pieces = stacked.reshape(stacked.shape[0], 3, rows, stacked.shape[-1])
    middle = pieces[:, 1]
    from_next = jnp.concatenate([pieces[1:, 0], jnp.zeros_like(pieces[:1, 0])], 0)
    from_prev = jnp.concatenate([jnp.zeros_like(pieces[:1, 2]), pieces[:-1, 2]], 0)
    return (middle + from_next + from_prev).reshape(-1, stacked.shape[-1])


def reference(video_query, video_key, video_value, video_cot, audio_query, audio_key, audio_value, audio_cot, intersection):
    score_scale = DH ** -0.5
    firsts = intersection[:, 0].astype(jnp.int32)
    lasts = intersection[:, 1].astype(jnp.int32)
    padded_firsts = jnp.pad(firsts, (1, 1), constant_values=BEYOND)
    padded_lasts = jnp.pad(lasts, (1, 1), constant_values=-1)

    def video_side(block_index):
        start = block_index * VTOK_DEV
        rows = (block_index - 1) * ATOK_DEV + jnp.arange(3 * ATOK_DEV, dtype=jnp.int32)
        present = (rows >= firsts[block_index]) & (rows < lasts[block_index])
        return attend(lax.dynamic_slice_in_dim(video_query, start, VTOK_DEV, 0),
                      window(audio_key, block_index, ATOK_DEV),
                      window(audio_value, block_index, ATOK_DEV),
                      lax.dynamic_slice_in_dim(video_cot, start, VTOK_DEV, 0),
                      present[None, :], score_scale)

    def audio_side(block_index):
        start = block_index * ATOK_DEV
        rows = start + jnp.arange(ATOK_DEV, dtype=jnp.int32)
        near_firsts = lax.dynamic_slice_in_dim(padded_firsts, block_index, 3, 0)
        near_lasts = lax.dynamic_slice_in_dim(padded_lasts, block_index, 3, 0)
        owner = jnp.arange(3 * VTOK_DEV, dtype=jnp.int32) // VTOK_DEV
        present = (rows[:, None] >= near_firsts[owner][None, :]) & (rows[:, None] < near_lasts[owner][None, :])
        return attend(lax.dynamic_slice_in_dim(audio_query, start, ATOK_DEV, 0),
                      window(video_key, block_index, VTOK_DEV),
                      window(video_value, block_index, VTOK_DEV),
                      lax.dynamic_slice_in_dim(audio_cot, start, ATOK_DEV, 0),
                      present, score_scale)

    blocks = jnp.arange(BLOCKS, dtype=jnp.int32)
    video_full, video_query_grad, audio_key_parts, audio_value_parts = lax.map(video_side, blocks)
    audio_full, audio_query_grad, video_key_parts, video_value_parts = lax.map(audio_side, blocks)
    width = H * DH
    video_out = video_full.reshape(-1, width).astype(jnp.bfloat16)
    audio_out = audio_full.reshape(-1, width).astype(jnp.bfloat16)
    video_query_grad = video_query_grad.reshape(-1, width).astype(jnp.bfloat16)
    audio_query_grad = audio_query_grad.reshape(-1, width).astype(jnp.bfloat16)
    audio_key_grad = fold_windows(audio_key_parts, ATOK_DEV).astype(jnp.bfloat16)
    audio_value_grad = fold_windows(audio_value_parts, ATOK_DEV).astype(jnp.bfloat16)
    video_key_grad = fold_windows(video_key_parts, VTOK_DEV).astype(jnp.bfloat16)
    video_value_grad = fold_windows(video_value_parts, VTOK_DEV).astype(jnp.bfloat16)
    return (video_out, audio_out, video_query_grad, video_key_grad, video_value_grad,
            audio_query_grad, audio_key_grad, audio_value_grad)
```

```python
import functools

import jax
import jax.numpy as jnp
from jax import lax
from jax.experimental import pallas as pl
from jax.experimental.pallas import tpu as pltpu
from jax.sharding import PartitionSpec as P

DH = 128
NEG = -1e30
LOG2E = 1.4426950408889634
MESH = pl.DeviceIdType.MESH
F32 = jnp.float32
BF16 = jnp.bfloat16
Q, K, V, C = 0, 1, 2, 3
DK, DV, OUT, DQ = 0, 1, 2, 3
CHUNKS = 3


def dot_nt(a, b):
    return lax.dot_general(a, b, (((1,), (1,)), ((), ())), preferred_element_type=F32)


def dot_nn(a, b):
    return lax.dot_general(a, b, (((1,), (0,)), ((), ())), preferred_element_type=F32)


def dot_tn(a, b):
    return lax.dot_general(a, b, (((0,), (0,)), ((), ())), preferred_element_type=F32)


def joined(parts):
    top = functools.reduce(jnp.maximum, [p[0] for p in parts])
    total = sum(p[1] * jnp.exp2(p[0] - top) for p in parts)
    weighted = sum(p[2] * jnp.exp2(p[0] - top) for p in parts)
    inverse = jnp.where(total > 0, 1.0 / jnp.where(total > 0, total, 1.0), 0.0)
    return jnp.exp2(parts[0][0] - top) * inverse, weighted * inverse


def kernel(blocks, vrows, arows, heads, *refs):
    (vq, vk, vv, vc, aq, ak, av, ac, inter, out) = refs[:10]
    (vid, win, e_on, dp_on, e_far, dp_far, p1, ds1, p2, ds2, own, s_near, s_far, r_near, r_far,
     es, ls, re_n, re_f, re_fn, rl_f, rl_nf, fac_on, fac_far, bias,
     load_sem, near_sem, far_ssem, far_rsem, es_ssem, es_rsem, ls_ssem, ls_rsem,
     kv_ssem, kv_rsem, oq_ssem, oq_rsem, nr_ssem, nr_rsem) = refs[10:]
    scale = DH ** (-0.5)
    scale2 = scale * LOG2E
    two = 2 * arows
    three = 3 * arows

    b = lax.axis_index("video")
    odd = lax.rem(b, 2)
    n = b + 1 - 2 * odd
    f = b - 1 + 2 * odd
    nf = n - 1 + 2 * (1 - odd)
    fn = f + 1 - 2 * (1 - odd)
    has_f = (f >= 0) & (f < blocks)
    has_nf = (nf >= 0) & (nf < blocks)

    def here(index):
        return {"video": index}

    barrier = pltpu.get_barrier_semaphore()
    pl.semaphore_signal(barrier, inc=1, device_id=here(n), device_id_type=MESH)

    @pl.when(has_f)
    def _():
        pl.semaphore_signal(barrier, inc=1, device_id=here(f), device_id_type=MESH)
        pl.semaphore_signal(barrier, inc=1, device_id=here(fn), device_id_type=MESH)

    @pl.when(has_nf)
    def _():
        pl.semaphore_signal(barrier, inc=1, device_id=here(nf), device_id_type=MESH)

    loads = []
    for t, ref in enumerate((aq, ak, av, ac)):
        loads.append(pltpu.make_async_copy(ref, win.at[t, pl.ds(0, arows)], load_sem.at[t]))
    for t, ref in enumerate((vq, vk, vv, vc)):
        loads.append(pltpu.make_async_copy(ref, vid.at[t], load_sem.at[4 + t]))
    for copy in loads:
        copy.start()

    first, last = inter[b, 0], inter[b, 1]
    lane = lax.broadcasted_iota(jnp.int32, (1, DH), 1)
    rows_on = jnp.where(lane < arows, b * arows + lane, n * arows + lane - arows)
    mask_on = (rows_on >= first) & (rows_on < last)
    lane_far = lax.broadcasted_iota(jnp.int32, (1, arows), 1)
    rows_far = f * arows + lane_far
    mask_far = (rows_far >= first) & (rows_far < last)
    sub = lax.broadcasted_iota(jnp.int32, (three, DH), 0)
    rows_sub = jnp.where(sub < arows, b * arows + sub,
                         jnp.where(sub < two, n * arows + sub - arows, f * arows + sub - two))
    bias[...] = jnp.where((rows_sub >= first) & (rows_sub < last), 0.0, NEG)

    es[...] = jnp.zeros_like(es)
    ls[...] = jnp.zeros_like(ls)

    @pl.when(jnp.logical_not(has_f))
    def _():
        for t in range(4):
            win[t, pl.ds(two, arows), :] = jnp.zeros((arows, heads * DH), BF16)
            r_far[t] = jnp.zeros((arows, heads * DH), BF16)
        for ref in (re_f, re_fn, rl_f):
            ref[0] = jnp.full(ref.shape[1:], NEG, F32)
            ref[1] = jnp.zeros(ref.shape[1:], F32)
            ref[2] = jnp.zeros(ref.shape[1:], F32)

    @pl.when(jnp.logical_not(has_nf))
    def _():
        rl_nf[0] = jnp.full(rl_nf.shape[1:], NEG, F32)
        rl_nf[1] = jnp.zeros(rl_nf.shape[1:], F32)
        rl_nf[2] = jnp.zeros(rl_nf.shape[1:], F32)

    def remote(src, dst, ssem, rsem, device):
        return pltpu.make_async_remote_copy(
            src_ref=src, dst_ref=dst, send_sem=ssem, recv_sem=rsem, device_id=here(device), device_id_type=MESH
        )

    per = heads // CHUNKS
    width = per * DH

    def chunk_cols(c):
        return pl.ds(c * width, width)

    near_in = remote(win.at[:, pl.ds(0, arows)], win.at[:, pl.ds(arows, arows)], near_sem.at[0], near_sem.at[1], n)
    far_in = [
        remote(win.at[:, pl.ds(0, arows), chunk_cols(c)], win.at[:, pl.ds(two, arows), chunk_cols(c)],
               far_ssem.at[c], far_rsem.at[c], f)
        for c in range(CHUNKS)
    ]
    es_n = remote(es, re_n, es_ssem.at[0], es_rsem.at[0], n)
    es_f = remote(es, re_f, es_ssem.at[1], es_rsem.at[1], f)
    es_nf = remote(es, re_fn, es_ssem.at[2], es_rsem.at[2], nf)
    ls_f = remote(ls, rl_f, ls_ssem.at[0], ls_rsem.at[0], f)
    ls_fn = remote(ls, rl_nf, ls_ssem.at[1], ls_rsem.at[1], fn)
    kv_far = [
        remote(s_far.at[pl.ds(0, 2), :, chunk_cols(c)], r_far.at[pl.ds(0, 2), :, chunk_cols(c)],
               kv_ssem.at[c], kv_rsem.at[c], f)
        for c in range(CHUNKS)
    ]
    oq_far = [
        remote(s_far.at[pl.ds(2, 2), :, chunk_cols(c)], r_far.at[pl.ds(2, 2), :, chunk_cols(c)],
               oq_ssem.at[c], oq_rsem.at[c], f)
        for c in range(CHUNKS)
    ]
    kv_near = remote(s_near.at[pl.ds(0, 2)], r_near.at[pl.ds(0, 2)], nr_ssem.at[0], nr_rsem.at[0], n)
    oq_near = remote(s_near.at[pl.ds(2, 2)], r_near.at[pl.ds(2, 2)], nr_ssem.at[1], nr_rsem.at[1], n)

    for copy in loads[:4]:
        copy.wait()
    pl.semaphore_wait(barrier, 1 + 2 * has_f.astype(jnp.int32) + has_nf.astype(jnp.int32))

    @pl.when(has_f)
    def _():
        for c in range(CHUNKS - 1):
            far_in[c].start()

    near_in.start()
    for copy in loads[4:]:
        copy.wait()
    near_in.wait_recv()

    for h in range(heads):
        cols = pl.ds(h * DH, DH)
        s = dot_nt(vid[K, :, cols], win[Q, pl.ds(0, two), cols]) * scale2
        dp = dot_nt(vid[V, :, cols], win[C, pl.ds(0, two), cols])
        top = jnp.max(s, axis=0, keepdims=True)
        e = jnp.exp2(s - top)
        e_on[h] = e
        dp_on[h] = dp
        es[0, pl.ds(h, 1), :] = jnp.where(mask_on, top, NEG)
        es[1, pl.ds(h, 1), :] = jnp.where(mask_on, jnp.sum(e, axis=0, keepdims=True), 0.0)
        es[2, pl.ds(h, 1), :] = jnp.where(mask_on, jnp.sum(e * dp, axis=0, keepdims=True), 0.0)

    @pl.when(has_f)
    def _():
        es_f.start()

    @pl.when(has_nf)
    def _():
        es_nf.start()

    es_n.start()

    @pl.when(has_f)
    def _():
        far_in[CHUNKS - 1].start()

    def stage_scores(c):
        @pl.when(has_f)
        def _():
            far_in[c].wait_recv()

        for h in range(c * per, (c + 1) * per):
            cols = pl.ds(h * DH, DH)
            qv, cv = vid[Q, :, cols], vid[C, :, cols]
            s = dot_nt(win[K, :, cols], qv) * scale2 + bias[...]
            dp = dot_nt(win[V, :, cols], cv)
            top = jnp.max(s, axis=0, keepdims=True)
            e = jnp.exp2(s - top)
            inverse = 1.0 / jnp.sum(e, axis=0, keepdims=True)
            prob = e * inverse
            delta = jnp.sum(prob * dp, axis=0, keepdims=True)
            weights = prob.astype(BF16)
            dscore = (prob * (dp - delta)).astype(BF16)
            p1[h] = weights
            ds1[h] = dscore
            s_far[DK, :, cols] = (dot_nn(dscore[two:], qv) * scale).astype(BF16)
            s_far[DV, :, cols] = dot_nn(weights[two:], cv).astype(BF16)

        @pl.when(has_f)
        def _():
            kv_far[c].start()

        for h in range(c * per, (c + 1) * per):
            cols = pl.ds(h * DH, DH)
            s = dot_nt(vid[K, :, cols], win[Q, pl.ds(two, arows), cols]) * scale2
            dp = dot_nt(vid[V, :, cols], win[C, pl.ds(two, arows), cols])
            top = jnp.max(s, axis=0, keepdims=True)
            e = jnp.exp2(s - top)
            e_far[h] = e
            dp_far[h] = dp
            ls[0, pl.ds(h, 1), pl.ds(0, arows)] = jnp.where(mask_far, top, NEG)
            ls[1, pl.ds(h, 1), pl.ds(0, arows)] = jnp.where(mask_far, jnp.sum(e, axis=0, keepdims=True), 0.0)
            ls[2, pl.ds(h, 1), pl.ds(0, arows)] = jnp.where(mask_far, jnp.sum(e * dp, axis=0, keepdims=True), 0.0)

    def wait_early():
        @pl.when(has_f)
        def _():
            es_f.wait_recv()
            es_nf.wait_recv()

    def stage_far(c):
        factor, delta = joined([
            [ls[i] for i in range(3)],
            [re_f[i] for i in range(3)],
            [pltpu.roll(re_fn[i], arows, 1) for i in range(3)],
        ])
        fac_far[0] = factor
        fac_far[1] = delta
        for h in range(c * per, (c + 1) * per):
            cols = pl.ds(h * DH, DH)
            prob = e_far[h] * fac_far[0, pl.ds(h, 1), pl.ds(0, arows)]
            weights = prob.astype(BF16)
            dscore = (prob * (dp_far[h] - fac_far[1, pl.ds(h, 1), pl.ds(0, arows)])).astype(BF16)
            p2[h, :, pl.ds(two, arows)] = weights
            ds2[h, :, pl.ds(two, arows)] = dscore
            s_far[OUT, :, cols] = dot_tn(weights, vid[V, :, cols]).astype(BF16)
            s_far[DQ, :, cols] = (dot_tn(dscore, vid[K, :, cols]) * scale).astype(BF16)

        @pl.when(has_f)
        def _():
            oq_far[c].start()

    stage_scores(0)
    stage_scores(1)
    wait_early()
    stage_far(0)
    stage_far(1)
    stage_scores(2)

    @pl.when(has_f)
    def _():
        ls_f.start()
        ls_fn.start()

    stage_far(2)

    for h in range(heads):
        cols = pl.ds(h * DH, DH)
        dk = dot_nn(ds1[h, pl.ds(0, two), :], vid[Q, :, cols]) * scale
        dv = dot_nn(p1[h, pl.ds(0, two), :], vid[C, :, cols])
        own[DK, :, cols] = dk[:arows]
        own[DV, :, cols] = dv[:arows]
        s_near[DK, :, cols] = dk[arows:].astype(BF16)
        s_near[DV, :, cols] = dv[arows:].astype(BF16)
    kv_near.start()

    def place(index):
        starts = [0, vrows, vrows + arows, 2 * vrows + arows, 3 * vrows + arows,
                  4 * vrows + arows, 4 * vrows + 2 * arows, 4 * vrows + 3 * arows]
        return pl.ds(starts[index], arows if index in (1, 5, 6, 7) else vrows)

    for h in range(heads):
        cols = pl.ds(h * DH, DH)
        out[place(0), cols] = dot_tn(p1[h], win[V, :, cols]).astype(BF16)
        out[place(2), cols] = (dot_tn(ds1[h], win[K, :, cols]) * scale).astype(BF16)

    es_n.wait_recv()

    @pl.when(has_f)
    def _():
        ls_f.wait_recv()

    @pl.when(has_nf)
    def _():
        ls_fn.wait_recv()

    left = lax.broadcasted_iota(jnp.int32, (8, DH), 1) < arows
    factor, delta = joined([
        [es[i] for i in range(3)],
        [pltpu.roll(re_n[i], arows, 1) for i in range(3)],
        [jnp.where(left, rl_f[i], pltpu.roll(rl_nf[i], arows, 1)) for i in range(3)],
    ])
    fac_on[0] = factor
    fac_on[1] = delta
    for h in range(heads):
        cols = pl.ds(h * DH, DH)
        prob = e_on[h] * fac_on[0, pl.ds(h, 1), :]
        weights = prob.astype(BF16)
        dscore = (prob * (dp_on[h] - fac_on[1, pl.ds(h, 1), :])).astype(BF16)
        p2[h, :, pl.ds(0, two)] = weights
        ds2[h, :, pl.ds(0, two)] = dscore
        o = dot_tn(weights, vid[V, :, cols])
        dq = dot_tn(dscore, vid[K, :, cols]) * scale
        own[OUT, :, cols] = o[:arows]
        own[DQ, :, cols] = dq[:arows]
        s_near[OUT, :, cols] = o[arows:].astype(BF16)
        s_near[DQ, :, cols] = dq[arows:].astype(BF16)
    oq_near.start()

    for h in range(heads):
        cols = pl.ds(h * DH, DH)
        out[place(3), cols] = (dot_nn(ds2[h, :, pl.ds(0, three)], win[Q, :, cols]) * scale).astype(BF16)
        out[place(4), cols] = dot_nn(p2[h, :, pl.ds(0, three)], win[C, :, cols]).astype(BF16)

    kv_near.wait_recv()
    oq_near.wait_recv()
    for c in range(CHUNKS):
        for pair, copies in (((DK, DV), kv_far), ((OUT, DQ), oq_far)):
            @pl.when(has_f)
            def _(copy=copies[c]):
                copy.wait_recv()

            for t in pair:
                cols = chunk_cols(c)
                total = own[t, :, cols] + r_near[t, :, cols].astype(F32) + r_far[t, :, cols].astype(F32)
                out[place({OUT: 1, DQ: 5, DK: 6, DV: 7}[t]), cols] = total.astype(BF16)

    near_in.wait_send()
    es_n.wait_send()
    kv_near.wait_send()
    oq_near.wait_send()

    @pl.when(has_f)
    def _():
        for copy in (*far_in, *kv_far, *oq_far, es_f, ls_f, ls_fn):
            copy.wait_send()

    @pl.when(has_nf)
    def _():
        es_nf.wait_send()


def spread(sizes, joint, *refs):
    outs, sems = refs[: len(sizes)], refs[len(sizes)]
    start, copies = 0, []
    for index, size in enumerate(sizes):
        copies.append(pltpu.make_async_copy(joint.at[pl.ds(start, size)], outs[index], sems.at[index]))
        start += size
    for copy in copies:
        copy.start()
    for copy in copies:
        copy.wait()


def local(video_query, video_key, video_value, video_cot, audio_query, audio_key, audio_value, audio_cot, intersection):
    vrows, features = video_query.shape
    arows = audio_query.shape[0]
    heads = features // DH
    blocks = lax.axis_size("video")
    sizes = [vrows, arows, vrows, vrows, vrows, arows, arows, arows]
    dma = pltpu.SemaphoreType.DMA
    audio = (4, arows, features)
    scratch = [
        pltpu.VMEM((4, vrows, features), BF16),
        pltpu.VMEM((4, 3 * arows, features), BF16),
        pltpu.VMEM((heads, vrows, 2 * arows), F32),
        pltpu.VMEM((heads, vrows, 2 * arows), F32),
        pltpu.VMEM((heads, vrows, arows), F32),
        pltpu.VMEM((heads, vrows, arows), F32),
        pltpu.VMEM((heads, 3 * arows, vrows), BF16),
        pltpu.VMEM((heads, 3 * arows, vrows), BF16),
        pltpu.VMEM((heads, vrows, 4 * arows), BF16),
        pltpu.VMEM((heads, vrows, 4 * arows), BF16),
        pltpu.VMEM(audio, F32),
        pltpu.VMEM(audio, BF16),
        pltpu.VMEM(audio, BF16),
        pltpu.VMEM(audio, BF16),
        pltpu.VMEM(audio, BF16),
        *[pltpu.VMEM((3, 8, DH), F32)] * 7,
        *[pltpu.VMEM((2, 8, DH), F32)] * 2,
        pltpu.VMEM((3 * arows, DH), F32),
        dma((8,)),
        dma((2,)),
        dma((CHUNKS,)),
        dma((CHUNKS,)),
        dma((3,)),
        dma((3,)),
        dma((2,)),
        dma((2,)),
        dma((CHUNKS,)),
        dma((CHUNKS,)),
        dma((CHUNKS,)),
        dma((CHUNKS,)),
        dma((2,)),
        dma((2,)),
    ]
    any_space = pl.BlockSpec(memory_space=pl.ANY)
    joint = pl.pallas_call(
        functools.partial(kernel, blocks, vrows, arows, heads),
        out_shape=pltpu.VMEM((sum(sizes), features), BF16),
        in_specs=[any_space] * 8 + [pl.BlockSpec(memory_space=pltpu.SMEM)],
        out_specs=pl.BlockSpec(memory_space=pltpu.VMEM),
        scratch_shapes=scratch,
        compiler_params=pltpu.CompilerParams(
            collective_id=0, has_side_effects=True, vmem_limit_bytes=24 * 1024 * 1024
        ),
        cost_estimate=pl.CostEstimate(
            flops=24 * heads * vrows * 3 * arows * DH, bytes_accessed=12 * (vrows + arows) * features, transcendentals=0
        ),
        name="cross_attention",
    )(video_query, video_key, video_value, video_cot, audio_query, audio_key, audio_value, audio_cot, intersection)
    joint = pltpu.with_memory_space_constraint(joint, pltpu.VMEM)
    return tuple(
        pl.pallas_call(
            functools.partial(spread, sizes),
            out_shape=[jax.ShapeDtypeStruct((size, features), BF16) for size in sizes],
            in_specs=[any_space],
            out_specs=[any_space] * len(sizes),
            scratch_shapes=[dma((len(sizes),))],
            name="spread",
        )(joint)
    )


def solution(mesh):
    rows = P(("clip", "video"), "audio")
    return jax.shard_map(
        local,
        mesh=mesh,
        in_specs=(rows,) * 8 + (P("clip", None),),
        out_specs=(rows,) * 8,
        check_vma=False,
    )
```

```python
import functools

import jax
import jax.numpy as jnp
from jax import lax
from jax.experimental import pallas as pl
from jax.experimental.pallas import tpu as pltpu
from jax.sharding import PartitionSpec as P

DH = 128
NEG = -1e30
LOG2E = 1.4426950408889634
MESH = pl.DeviceIdType.MESH
F32 = jnp.float32
BF16 = jnp.bfloat16
Q, K, V, C = 0, 1, 2, 3
DK, DV, OUT, DQ = 0, 1, 2, 3
CHUNKS = 3


def dot_nt(a, b):
    return lax.dot_general(a, b, (((1,), (1,)), ((), ())), preferred_element_type=F32)


def dot_nn(a, b):
    return lax.dot_general(a, b, (((1,), (0,)), ((), ())), preferred_element_type=F32)


def dot_tn(a, b):
    return lax.dot_general(a, b, (((0,), (0,)), ((), ())), preferred_element_type=F32)


def joined(parts):
    top = functools.reduce(jnp.maximum, [p[0] for p in parts])
    total = sum(p[1] * jnp.exp2(p[0] - top) for p in parts)
    weighted = sum(p[2] * jnp.exp2(p[0] - top) for p in parts)
    inverse = jnp.where(total > 0, 1.0 / jnp.where(total > 0, total, 1.0), 0.0)
    return jnp.exp2(parts[0][0] - top) * inverse, weighted * inverse


def kernel(blocks, vrows, arows, heads, *refs):
    (vq, vk, vv, vc, aq, ak, av, ac, inter, out) = refs[:10]
    (spans, vid, win, e_on, dp_on, e_far, dp_far, p1, ds1, p2, ds2, own, s_near, s_far, r_near, r_far,
     es, ls, re_n, re_f, re_fn, rl_f, rl_nf, fac_on, fac_far, bias,
     load_sem, near_sem, far_ssem, far_rsem, es_ssem, es_rsem, ls_ssem, ls_rsem,
     kv_ssem, kv_rsem, oq_ssem, oq_rsem, nr_ssem, nr_rsem) = refs[10:]
    scale = DH ** (-0.5)
    scale2 = scale * LOG2E
    two = 2 * arows
    three = 3 * arows

    b = lax.axis_index("video")
    odd = lax.rem(b, 2)
    n = b + 1 - 2 * odd
    f = b - 1 + 2 * odd
    nf = n - 1 + 2 * (1 - odd)
    fn = f + 1 - 2 * (1 - odd)
    has_f = (f >= 0) & (f < blocks)
    has_nf = (nf >= 0) & (nf < blocks)

    def here(index):
        return {"video": index}

    barrier = pltpu.get_barrier_semaphore()
    pl.semaphore_signal(barrier, inc=1, device_id=here(n), device_id_type=MESH)

    @pl.when(has_f)
    def _():
        pl.semaphore_signal(barrier, inc=1, device_id=here(f), device_id_type=MESH)
        pl.semaphore_signal(barrier, inc=1, device_id=here(fn), device_id_type=MESH)

    @pl.when(has_nf)
    def _():
        pl.semaphore_signal(barrier, inc=1, device_id=here(nf), device_id_type=MESH)

    span_load = pltpu.make_async_copy(inter, spans, load_sem.at[8])
    span_load.start()
    loads = []
    for t, ref in enumerate((aq, ak, av, ac)):
        loads.append(pltpu.make_async_copy(ref, win.at[t, pl.ds(0, arows)], load_sem.at[t]))
    for t, ref in enumerate((vq, vk, vv, vc)):
        loads.append(pltpu.make_async_copy(ref, vid.at[t], load_sem.at[4 + t]))
    for copy in loads:
        copy.start()

    span_load.wait()
    first, last = spans[0, b], spans[1, b]
    lane = lax.broadcasted_iota(jnp.int32, (1, DH), 1)
    rows_on = jnp.where(lane < arows, b * arows + lane, n * arows + lane - arows)
    mask_on = (rows_on >= first) & (rows_on < last)
    lane_far = lax.broadcasted_iota(jnp.int32, (1, arows), 1)
    rows_far = f * arows + lane_far
    mask_far = (rows_far >= first) & (rows_far < last)
    sub = lax.broadcasted_iota(jnp.int32, (three, DH), 0)
    rows_sub = jnp.where(sub < arows, b * arows + sub,
                         jnp.where(sub < two, n * arows + sub - arows, f * arows + sub - two))
    bias[...] = jnp.where((rows_sub >= first) & (rows_sub < last), 0.0, NEG)

    es[...] = jnp.zeros_like(es)
    ls[...] = jnp.zeros_like(ls)

    @pl.when(jnp.logical_not(has_f))
    def _():
        for t in range(4):
            win[t, pl.ds(two, arows), :] = jnp.zeros((arows, heads * DH), BF16)
            r_far[t] = jnp.zeros((arows, heads * DH), BF16)
        for ref in (re_f, re_fn, rl_f):
            ref[0] = jnp.full(ref.shape[1:], NEG, F32)
            ref[1] = jnp.zeros(ref.shape[1:], F32)
            ref[2] = jnp.zeros(ref.shape[1:], F32)

    @pl.when(jnp.logical_not(has_nf))
    def _():
        rl_nf[0] = jnp.full(rl_nf.shape[1:], NEG, F32)
        rl_nf[1] = jnp.zeros(rl_nf.shape[1:], F32)
        rl_nf[2] = jnp.zeros(rl_nf.shape[1:], F32)

    def remote(src, dst, ssem, rsem, device):
        return pltpu.make_async_remote_copy(
            src_ref=src, dst_ref=dst, send_sem=ssem, recv_sem=rsem, device_id=here(device), device_id_type=MESH
        )

    per = heads // CHUNKS
    width = per * DH

    def chunk_cols(c):
        return pl.ds(c * width, width)

    near_in = remote(win.at[:, pl.ds(0, arows)], win.at[:, pl.ds(arows, arows)], near_sem.at[0], near_sem.at[1], n)
    far_in = [
        remote(win.at[:, pl.ds(0, arows), chunk_cols(c)], win.at[:, pl.ds(two, arows), chunk_cols(c)],
               far_ssem.at[c], far_rsem.at[c], f)
        for c in range(CHUNKS)
    ]
    es_n = remote(es, re_n, es_ssem.at[0], es_rsem.at[0], n)
    es_f = remote(es, re_f, es_ssem.at[1], es_rsem.at[1], f)
    es_nf = remote(es, re_fn, es_ssem.at[2], es_rsem.at[2], nf)
    ls_f = remote(ls, rl_f, ls_ssem.at[0], ls_rsem.at[0], f)
    ls_fn = remote(ls, rl_nf, ls_ssem.at[1], ls_rsem.at[1], fn)
    kv_far = [
        remote(s_far.at[pl.ds(0, 2), :, chunk_cols(c)], r_far.at[pl.ds(0, 2), :, chunk_cols(c)],
               kv_ssem.at[c], kv_rsem.at[c], f)
        for c in range(CHUNKS)
    ]
    oq_far = [
        remote(s_far.at[pl.ds(2, 2), :, chunk_cols(c)], r_far.at[pl.ds(2, 2), :, chunk_cols(c)],
               oq_ssem.at[c], oq_rsem.at[c], f)
        for c in range(CHUNKS)
    ]
    kv_near = remote(s_near.at[pl.ds(0, 2)], r_near.at[pl.ds(0, 2)], nr_ssem.at[0], nr_rsem.at[0], n)
    oq_near = remote(s_near.at[pl.ds(2, 2)], r_near.at[pl.ds(2, 2)], nr_ssem.at[1], nr_rsem.at[1], n)

    for copy in loads[:4]:
        copy.wait()
    pl.semaphore_wait(barrier, 1 + 2 * has_f.astype(jnp.int32) + has_nf.astype(jnp.int32))

    @pl.when(has_f)
    def _():
        for c in range(CHUNKS - 1):
            far_in[c].start()

    near_in.start()
    for copy in loads[4:]:
        copy.wait()
    near_in.wait_recv()

    for h in range(heads):
        cols = pl.ds(h * DH, DH)
        s = dot_nt(vid[K, :, cols], win[Q, pl.ds(0, two), cols]) * scale2
        dp = dot_nt(vid[V, :, cols], win[C, pl.ds(0, two), cols])
        top = jnp.max(s, axis=0, keepdims=True)
        e = jnp.exp2(s - top)
        e_on[h] = e
        dp_on[h] = dp
        es[0, pl.ds(h, 1), :] = jnp.where(mask_on, top, NEG)
        es[1, pl.ds(h, 1), :] = jnp.where(mask_on, jnp.sum(e, axis=0, keepdims=True), 0.0)
        es[2, pl.ds(h, 1), :] = jnp.where(mask_on, jnp.sum(e * dp, axis=0, keepdims=True), 0.0)

    @pl.when(has_f)
    def _():
        es_f.start()

    @pl.when(has_nf)
    def _():
        es_nf.start()

    es_n.start()

    @pl.when(has_f)
    def _():
        far_in[CHUNKS - 1].start()

    def stage_scores(c):
        @pl.when(has_f)
        def _():
            far_in[c].wait_recv()

        for h in range(c * per, (c + 1) * per):
            cols = pl.ds(h * DH, DH)
            qv, cv = vid[Q, :, cols], vid[C, :, cols]
            s = dot_nt(win[K, :, cols], qv) * scale2 + bias[...]
            dp = dot_nt(win[V, :, cols], cv)
            top = jnp.max(s, axis=0, keepdims=True)
            e = jnp.exp2(s - top)
            inverse = 1.0 / jnp.sum(e, axis=0, keepdims=True)
            prob = e * inverse
            delta = jnp.sum(prob * dp, axis=0, keepdims=True)
            weights = prob.astype(BF16)
            dscore = (prob * (dp - delta)).astype(BF16)
            p1[h] = weights
            ds1[h] = dscore
            s_far[DK, :, cols] = (dot_nn(dscore[two:], qv) * scale).astype(BF16)
            s_far[DV, :, cols] = dot_nn(weights[two:], cv).astype(BF16)

        @pl.when(has_f)
        def _():
            kv_far[c].start()

        for h in range(c * per, (c + 1) * per):
            cols = pl.ds(h * DH, DH)
            s = dot_nt(vid[K, :, cols], win[Q, pl.ds(two, arows), cols]) * scale2
            dp = dot_nt(vid[V, :, cols], win[C, pl.ds(two, arows), cols])
            top = jnp.max(s, axis=0, keepdims=True)
            e = jnp.exp2(s - top)
            e_far[h] = e
            dp_far[h] = dp
            ls[0, pl.ds(h, 1), pl.ds(0, arows)] = jnp.where(mask_far, top, NEG)
            ls[1, pl.ds(h, 1), pl.ds(0, arows)] = jnp.where(mask_far, jnp.sum(e, axis=0, keepdims=True), 0.0)
            ls[2, pl.ds(h, 1), pl.ds(0, arows)] = jnp.where(mask_far, jnp.sum(e * dp, axis=0, keepdims=True), 0.0)

    def wait_early():
        @pl.when(has_f)
        def _():
            es_f.wait_recv()
            es_nf.wait_recv()

    def stage_far(c):
        factor, delta = joined([
            [ls[i] for i in range(3)],
            [re_f[i] for i in range(3)],
            [pltpu.roll(re_fn[i], arows, 1) for i in range(3)],
        ])
        fac_far[0] = factor
        fac_far[1] = delta
        for h in range(c * per, (c + 1) * per):
            cols = pl.ds(h * DH, DH)
            prob = e_far[h] * fac_far[0, pl.ds(h, 1), pl.ds(0, arows)]
            weights = prob.astype(BF16)
            dscore = (prob * (dp_far[h] - fac_far[1, pl.ds(h, 1), pl.ds(0, arows)])).astype(BF16)
            p2[h, :, pl.ds(two, arows)] = weights
            ds2[h, :, pl.ds(two, arows)] = dscore
            s_far[OUT, :, cols] = dot_tn(weights, vid[V, :, cols]).astype(BF16)
            s_far[DQ, :, cols] = (dot_tn(dscore, vid[K, :, cols]) * scale).astype(BF16)

        @pl.when(has_f)
        def _():
            oq_far[c].start()

    stage_scores(0)
    stage_scores(1)
    wait_early()
    stage_far(0)
    stage_far(1)
    stage_scores(2)

    @pl.when(has_f)
    def _():
        ls_f.start()
        ls_fn.start()

    stage_far(2)

    for h in range(heads):
        cols = pl.ds(h * DH, DH)
        dk = dot_nn(ds1[h, pl.ds(0, two), :], vid[Q, :, cols]) * scale
        dv = dot_nn(p1[h, pl.ds(0, two), :], vid[C, :, cols])
        own[DK, :, cols] = dk[:arows]
        own[DV, :, cols] = dv[:arows]
        s_near[DK, :, cols] = dk[arows:].astype(BF16)
        s_near[DV, :, cols] = dv[arows:].astype(BF16)
    kv_near.start()

    def place(index):
        starts = [0, vrows, vrows + arows, 2 * vrows + arows, 3 * vrows + arows,
                  4 * vrows + arows, 4 * vrows + 2 * arows, 4 * vrows + 3 * arows]
        return pl.ds(starts[index], arows if index in (1, 5, 6, 7) else vrows)

    for h in range(heads):
        cols = pl.ds(h * DH, DH)
        out[place(0), cols] = dot_tn(p1[h], win[V, :, cols]).astype(BF16)
        out[place(2), cols] = (dot_tn(ds1[h], win[K, :, cols]) * scale).astype(BF16)

    es_n.wait_recv()

    @pl.when(has_f)
    def _():
        ls_f.wait_recv()

    @pl.when(has_nf)
    def _():
        ls_fn.wait_recv()

    left = lax.broadcasted_iota(jnp.int32, (8, DH), 1) < arows
    factor, delta = joined([
        [es[i] for i in range(3)],
        [pltpu.roll(re_n[i], arows, 1) for i in range(3)],
        [jnp.where(left, rl_f[i], pltpu.roll(rl_nf[i], arows, 1)) for i in range(3)],
    ])
    fac_on[0] = factor
    fac_on[1] = delta
    for h in range(heads):
        cols = pl.ds(h * DH, DH)
        prob = e_on[h] * fac_on[0, pl.ds(h, 1), :]
        weights = prob.astype(BF16)
        dscore = (prob * (dp_on[h] - fac_on[1, pl.ds(h, 1), :])).astype(BF16)
        p2[h, :, pl.ds(0, two)] = weights
        ds2[h, :, pl.ds(0, two)] = dscore
        o = dot_tn(weights, vid[V, :, cols])
        dq = dot_tn(dscore, vid[K, :, cols]) * scale
        own[OUT, :, cols] = o[:arows]
        own[DQ, :, cols] = dq[:arows]
        s_near[OUT, :, cols] = o[arows:].astype(BF16)
        s_near[DQ, :, cols] = dq[arows:].astype(BF16)
    oq_near.start()

    for h in range(heads):
        cols = pl.ds(h * DH, DH)
        out[place(3), cols] = (dot_nn(ds2[h, :, pl.ds(0, three)], win[Q, :, cols]) * scale).astype(BF16)
        out[place(4), cols] = dot_nn(p2[h, :, pl.ds(0, three)], win[C, :, cols]).astype(BF16)

    kv_near.wait_recv()
    oq_near.wait_recv()
    for c in range(CHUNKS):
        for pair, copies in (((DK, DV), kv_far), ((OUT, DQ), oq_far)):
            @pl.when(has_f)
            def _(copy=copies[c]):
                copy.wait_recv()

            for t in pair:
                cols = chunk_cols(c)
                total = own[t, :, cols] + r_near[t, :, cols].astype(F32) + r_far[t, :, cols].astype(F32)
                out[place({OUT: 1, DQ: 5, DK: 6, DV: 7}[t]), cols] = total.astype(BF16)

    near_in.wait_send()
    es_n.wait_send()
    kv_near.wait_send()
    oq_near.wait_send()

    @pl.when(has_f)
    def _():
        for copy in (*far_in, *kv_far, *oq_far, es_f, ls_f, ls_fn):
            copy.wait_send()

    @pl.when(has_nf)
    def _():
        es_nf.wait_send()


def spread(sizes, joint, *refs):
    outs, sems = refs[: len(sizes)], refs[len(sizes)]
    start, copies = 0, []
    for index, size in enumerate(sizes):
        copies.append(pltpu.make_async_copy(joint.at[pl.ds(start, size)], outs[index], sems.at[index]))
        start += size
    for copy in copies:
        copy.start()
    for copy in copies:
        copy.wait()


def local(video_query, video_key, video_value, video_cot, audio_query, audio_key, audio_value, audio_cot, intersection):
    vrows, features = video_query.shape
    arows = audio_query.shape[0]
    heads = features // DH
    blocks = lax.axis_size("video")
    sizes = [vrows, arows, vrows, vrows, vrows, arows, arows, arows]
    dma = pltpu.SemaphoreType.DMA
    audio = (4, arows, features)
    scratch = [
        pltpu.SMEM((2, blocks), jnp.int32),
        pltpu.VMEM((4, vrows, features), BF16),
        pltpu.VMEM((4, 3 * arows, features), BF16),
        pltpu.VMEM((heads, vrows, 2 * arows), F32),
        pltpu.VMEM((heads, vrows, 2 * arows), F32),
        pltpu.VMEM((heads, vrows, arows), F32),
        pltpu.VMEM((heads, vrows, arows), F32),
        pltpu.VMEM((heads, 3 * arows, vrows), BF16),
        pltpu.VMEM((heads, 3 * arows, vrows), BF16),
        pltpu.VMEM((heads, vrows, 4 * arows), BF16),
        pltpu.VMEM((heads, vrows, 4 * arows), BF16),
        pltpu.VMEM(audio, F32),
        pltpu.VMEM(audio, BF16),
        pltpu.VMEM(audio, BF16),
        pltpu.VMEM(audio, BF16),
        pltpu.VMEM(audio, BF16),
        *[pltpu.VMEM((3, 8, DH), F32)] * 7,
        *[pltpu.VMEM((2, 8, DH), F32)] * 2,
        pltpu.VMEM((3 * arows, DH), F32),
        dma((9,)),
        dma((2,)),
        dma((CHUNKS,)),
        dma((CHUNKS,)),
        dma((3,)),
        dma((3,)),
        dma((2,)),
        dma((2,)),
        dma((CHUNKS,)),
        dma((CHUNKS,)),
        dma((CHUNKS,)),
        dma((CHUNKS,)),
        dma((2,)),
        dma((2,)),
    ]
    any_space = pl.BlockSpec(memory_space=pl.ANY)
    in_hbm = pl.BlockSpec(memory_space=pltpu.HBM)
    joint = pl.pallas_call(
        functools.partial(kernel, blocks, vrows, arows, heads),
        out_shape=pltpu.VMEM((sum(sizes), features), BF16),
        in_specs=[in_hbm] * 9,
        out_specs=pl.BlockSpec(memory_space=pltpu.VMEM),
        scratch_shapes=scratch,
        compiler_params=pltpu.CompilerParams(
            collective_id=0, has_side_effects=True, vmem_limit_bytes=24 * 1024 * 1024
        ),
        cost_estimate=pl.CostEstimate(
            flops=24 * heads * vrows * 3 * arows * DH, bytes_accessed=12 * (vrows + arows) * features, transcendentals=0
        ),
        name="cross_attention",
    )(*[pltpu.with_memory_space_constraint(x, pltpu.HBM) for x in (video_query, video_key, video_value, video_cot, audio_query, audio_key, audio_value, audio_cot, jnp.transpose(intersection))])
    joint = pltpu.with_memory_space_constraint(joint, pltpu.VMEM)
    return tuple(
        pl.pallas_call(
            functools.partial(spread, sizes),
            out_shape=[jax.ShapeDtypeStruct((size, features), BF16) for size in sizes],
            in_specs=[any_space],
            out_specs=[any_space] * len(sizes),
            scratch_shapes=[dma((len(sizes),))],
            name="spread",
        )(joint)
    )


def solution(mesh):
    rows = P(("clip", "video"), "audio")
    return jax.shard_map(
        local,
        mesh=mesh,
        in_specs=(rows,) * 8 + (P("clip", None),),
        out_specs=(rows,) * 8,
        check_vma=False,
    )
```

```python
import functools

import jax
import jax.numpy as jnp
from jax import lax
from jax.experimental import pallas as pl
from jax.experimental.pallas import tpu as pltpu
from jax.sharding import PartitionSpec as P

DH = 128
NEG = -1e30
ABSENT = -2e30
LOG2E = 1.4426950408889634
MESH = pl.DeviceIdType.MESH
F32 = jnp.float32
BF16 = jnp.bfloat16
Q, K, V, C = 0, 1, 2, 3
DK, DV, OUT, DQ = 0, 1, 2, 3
FIRST = ((K, 1), (V, 1), (Q, 0), (C, 0), (Q, 1), (C, 1))
LATER = ((Q, 2), (C, 2), (K, 2), (V, 2))


def dot_nt(a, b):
    return lax.dot_general(a, b, (((1,), (1,)), ((), ())), preferred_element_type=F32)


def dot_nn(a, b):
    return lax.dot_general(a, b, (((1,), (0,)), ((), ())), preferred_element_type=F32)


def dot_tn(a, b):
    return lax.dot_general(a, b, (((0,), (0,)), ((), ())), preferred_element_type=F32)


def joined(top_here, parts):
    top = functools.reduce(jnp.maximum, [p[0] for p in parts])
    shares = [jnp.exp2(p[0] - top) for p in parts]
    inverse = 1.0 / sum(shares)
    return jnp.exp2(top_here - top) * inverse, sum(w * p[1] for w, p in zip(shares, parts)) * inverse


def kernel(blocks, vrows, arows, heads, *refs):
    (vq, vk, vv, vc, aq, ak, av, ac, inter, out) = refs[:10]
    (spans, vqc, vkv, qc, win, qb, e_on, dp_on, e_far, dp_far, p1, ds1, p2, ds2, own_a, own_v,
     s_near, r_near, s_video, r_video, s_far, r_far, es, ls, re_f, rl_f, m_on, m_far, bias,
     load_sem, near_ssem, near_rsem, far_ssem, far_rsem, st_ssem, st_rsem,
     kv_ssem, kv_rsem, oq_ssem, oq_rsem, nr_ssem, nr_rsem) = refs[10:]
    scale = DH ** (-0.5)
    scale2 = scale * LOG2E
    two = 2 * arows
    three = 3 * arows
    pairs = heads // 2
    wide = 2 * DH

    b = lax.axis_index("video")
    odd = lax.rem(b, 2)
    n = b + 1 - 2 * odd
    f = b - 1 + 2 * odd
    has_f = (f >= 0) & (f < blocks)

    def here(index):
        return {"video": index}

    barrier = pltpu.get_barrier_semaphore()

    @pl.when(has_f)
    def _():
        pl.semaphore_signal(barrier, inc=1, device_id=here(f), device_id_type=MESH)

    pl.semaphore_signal(barrier, inc=1, device_id=here(n), device_id_type=MESH)

    span_load = pltpu.make_async_copy(inter, spans, load_sem.at[8])
    loads = [
        pltpu.make_async_copy(vk, vkv.at[0, pl.ds(0, vrows)], load_sem.at[0]),
        pltpu.make_async_copy(vv, vkv.at[1, pl.ds(0, vrows)], load_sem.at[1]),
        pltpu.make_async_copy(aq, qc.at[0, pl.ds(0, arows)], load_sem.at[2]),
        pltpu.make_async_copy(ac, qc.at[1, pl.ds(0, arows)], load_sem.at[3]),
        pltpu.make_async_copy(ak, win.at[0, pl.ds(0, arows)], load_sem.at[4]),
        pltpu.make_async_copy(av, win.at[1, pl.ds(0, arows)], load_sem.at[5]),
        pltpu.make_async_copy(vq, vqc.at[0], load_sem.at[6]),
        pltpu.make_async_copy(vc, vqc.at[1], load_sem.at[7]),
    ]
    for copy in (span_load, *loads):
        copy.start()

    def remote(src, dst, ssem, rsem, device):
        return pltpu.make_async_remote_copy(
            src_ref=src, dst_ref=dst, send_sem=ssem, recv_sem=rsem, device_id=here(device), device_id_type=MESH
        )

    def pair_cols(p):
        return pl.ds(p * wide, wide)

    def head_cols(h):
        return pl.ds(h * DH, DH)

    near_in = [
        remote(ref, dst, near_ssem.at[t], near_rsem.at[t], n)
        for t, (ref, dst) in enumerate((
            (vk, vkv.at[0, pl.ds(vrows, vrows)]),
            (vv, vkv.at[1, pl.ds(vrows, vrows)]),
            (ak, win.at[0, pl.ds(arows, arows)]),
            (av, win.at[1, pl.ds(arows, arows)]),
        ))
    ]
    far_in = [
        [remote(ref.at[:, pair_cols(p)], dst.at[:, pair_cols(p)], far_ssem.at[t, p], far_rsem.at[t, p], f)
         for p in range(pairs)]
        for t, (ref, dst) in enumerate((
            (aq, qc.at[0, pl.ds(arows, arows)]),
            (ak, win.at[0, pl.ds(two, arows)]),
            (av, win.at[1, pl.ds(two, arows)]),
            (ac, qc.at[1, pl.ds(arows, arows)]),
        ))
    ]
    es_f = remote(es, re_f, st_ssem.at[0], st_rsem.at[0], f)
    ls_f = remote(ls, rl_f, st_ssem.at[1], st_rsem.at[1], f)
    kv_far = [
        remote(s_far.at[pl.ds(0, 2), :, pair_cols(p)], r_far.at[pl.ds(0, 2), :, pair_cols(p)],
               kv_ssem.at[p], kv_rsem.at[p], f)
        for p in range(pairs)
    ]
    oq_far = [
        remote(s_far.at[pl.ds(2, 2), :, pair_cols(p)], r_far.at[pl.ds(2, 2), :, pair_cols(p)],
               oq_ssem.at[p], oq_rsem.at[p], f)
        for p in range(pairs)
    ]
    kv_near = remote(s_near, r_near, nr_ssem.at[pairs], nr_rsem.at[pairs], n)
    kv_video = [
        remote(s_video.at[:, :, pair_cols(p)], r_video.at[:, :, pair_cols(p)], nr_ssem.at[p], nr_rsem.at[p], n)
        for p in range(pairs)
    ]

    for p in range(pairs):
        for t in range(2):
            for half in range(2):
                rows = pl.ds(half * two, two)
                qb[t, p, rows, :] = jnp.zeros((two, wide), BF16)

    for ref in (es, ls, m_on, m_far):
        ref[...] = jnp.zeros_like(ref)

    pl.semaphore_wait(barrier, 1 + has_f.astype(jnp.int32))

    @pl.when(has_f)
    def _():
        far_in[K][0].start()
        far_in[V][0].start()

    for copy in near_in:
        copy.start()

    @pl.when(has_f)
    def _():
        for t, p in FIRST:
            far_in[t][p].start()

    span_load.wait()
    first, last = spans[0, b], spans[1, b]
    lane = lax.broadcasted_iota(jnp.int32, (1, two), 1)
    lane = jnp.where(lane < arows, lane, lane - arows)
    mask_far = (f * arows + lane >= first) & (f * arows + lane < last)
    mask_near = (b * arows + lane >= spans[0, n]) & (b * arows + lane < spans[1, n])
    bias_near = jnp.where(mask_near, 0.0, NEG)
    sub = lax.broadcasted_iota(jnp.int32, (three, vrows), 0)
    rows_sub = jnp.where(sub < arows, b * arows + sub,
                         jnp.where(sub < two, n * arows + sub - arows, f * arows + sub - two))
    bias[...] = jnp.where((rows_sub >= first) & (rows_sub < last), 0.0, NEG)

    @pl.when(jnp.logical_not(has_f))
    def _():
        for t in range(2):
            win[t, pl.ds(two, arows), :] = jnp.zeros((arows, heads * DH), BF16)
            qc[t, pl.ds(arows, arows), :] = jnp.zeros((arows, heads * DH), BF16)
        for t in range(4):
            r_far[t] = jnp.zeros((arows, heads * DH), BF16)
        for ref in (re_f, rl_f):
            ref[0] = jnp.full(ref.shape[1:], NEG, F32)
            ref[1] = jnp.zeros(ref.shape[1:], F32)

    for copy in loads:
        copy.wait()

    def place_blocks(p, start):
        for t in range(2):
            for k in range(2):
                qb[t, p, pl.ds(2 * start + k * arows, arows), head_cols(k)] = (
                    qc[t, pl.ds(start, arows), head_cols(2 * p + k)]
                )

    for p in range(pairs):
        place_blocks(p, 0)

    near_in[0].wait_recv()
    near_in[1].wait_recv()

    for p in range(pairs):
        s = dot_nt(vkv[0, :, pair_cols(p)], qb[0, p, pl.ds(0, two), :]) * scale2
        dp = dot_nt(vkv[1, :, pair_cols(p)], qb[1, p, pl.ds(0, two), :])
        s = jnp.concatenate([s[:vrows], s[vrows:] + bias_near], axis=0)
        top = jnp.max(s, axis=0, keepdims=True)
        e = jnp.exp2(s - top)
        e_on[p] = e
        dp_on[p] = dp
        total = jnp.sum(e, axis=0, keepdims=True)
        m_on[pl.ds(p, 1), :] = top
        es[0, pl.ds(p, 1), :] = top + jnp.log(total) * LOG2E
        es[1, pl.ds(p, 1), :] = jnp.sum(e * dp, axis=0, keepdims=True) / total

    @pl.when(has_f)
    def _():
        es_f.start()
        for t, p in LATER:
            far_in[t][p].start()

    near_in[2].wait_recv()
    near_in[3].wait_recv()

    def stage_scores(p):
        @pl.when(has_f)
        def _():
            far_in[K][p].wait_recv()
            far_in[V][p].wait_recv()

        for h in (2 * p, 2 * p + 1):
            cols = head_cols(h)
            qv, cv = vqc[0, :, cols], vqc[1, :, cols]
            s = dot_nt(win[0, :, cols], qv) * scale2 + bias[...]
            dp = dot_nt(win[1, :, cols], cv)
            top = jnp.max(s, axis=0, keepdims=True)
            e = jnp.exp2(s - top)
            inverse = 1.0 / jnp.sum(e, axis=0, keepdims=True)
            prob = e * inverse
            delta = jnp.sum(prob * dp, axis=0, keepdims=True)
            weights = prob.astype(BF16)
            dscore = (prob * (dp - delta)).astype(BF16)
            p1[h] = weights
            ds1[h] = dscore
            s_far[DK, :, cols] = (dot_nn(dscore[two:], qv) * scale).astype(BF16)
            s_far[DV, :, cols] = dot_nn(weights[two:], cv).astype(BF16)

        @pl.when(has_f)
        def _():
            kv_far[p].start()

    def stage_terms(p):
        @pl.when(has_f)
        def _():
            far_in[Q][p].wait_recv()
            far_in[C][p].wait_recv()

        place_blocks(p, arows)
        s = dot_nt(vkv[0, pl.ds(0, vrows), pair_cols(p)], qb[0, p, pl.ds(two, two), :]) * scale2
        dp = dot_nt(vkv[1, pl.ds(0, vrows), pair_cols(p)], qb[1, p, pl.ds(two, two), :])
        top = jnp.max(s, axis=0, keepdims=True)
        e = jnp.exp2(s - top)
        e_far[p] = e
        dp_far[p] = dp
        total = jnp.sum(e, axis=0, keepdims=True)
        m_far[pl.ds(p, 1), :] = jnp.where(mask_far, top, ABSENT)
        ls[0, pl.ds(p, 1), :] = jnp.where(mask_far, top + jnp.log(total) * LOG2E, NEG)
        ls[1, pl.ds(p, 1), :] = jnp.where(mask_far, jnp.sum(e * dp, axis=0, keepdims=True) / total, 0.0)

    def terms_of(ref, p):
        return [ref[0, pl.ds(p, 1), :], ref[1, pl.ds(p, 1), :]]

    def stage_far(p):
        factor, delta = joined(m_far[pl.ds(p, 1), :], [terms_of(ls, p), terms_of(re_f, p)])
        prob = e_far[p] * factor
        weights = prob.astype(BF16)
        dscore = (prob * (dp_far[p] - delta)).astype(BF16)
        p2[p, :, pl.ds(two, two)] = weights
        ds2[p, :, pl.ds(two, two)] = dscore
        weights, dscore = weights.T, dscore.T
        for k in range(2):
            cols = head_cols(2 * p + k)
            rows = slice(k * arows, (k + 1) * arows)
            s_far[OUT, :, cols] = dot_nn(weights[rows], vkv[1, pl.ds(0, vrows), cols]).astype(BF16)
            s_far[DQ, :, cols] = (dot_nn(dscore[rows], vkv[0, pl.ds(0, vrows), cols]) * scale).astype(BF16)

        @pl.when(has_f)
        def _():
            oq_far[p].start()

    stage_scores(0)
    stage_scores(1)
    stage_terms(0)

    @pl.when(has_f)
    def _():
        es_f.wait_recv()

    stage_far(0)
    stage_terms(1)
    stage_terms(2)

    @pl.when(has_f)
    def _():
        ls_f.start()

    stage_far(1)
    stage_far(2)
    stage_scores(2)

    for h in range(heads):
        cols = head_cols(h)
        dk = dot_nn(ds1[h, pl.ds(0, two), :], vqc[0, :, cols]) * scale
        dv = dot_nn(p1[h, pl.ds(0, two), :], vqc[1, :, cols])
        own_a[DK, :, cols] = dk[:arows]
        own_a[DV, :, cols] = dv[:arows]
        s_near[DK, :, cols] = dk[arows:].astype(BF16)
        s_near[DV, :, cols] = dv[arows:].astype(BF16)
    kv_near.start()

    def place(index):
        starts = [0, vrows, vrows + arows, 2 * vrows + arows, 3 * vrows + arows,
                  4 * vrows + arows, 4 * vrows + 2 * arows, 4 * vrows + 3 * arows]
        return pl.ds(starts[index], arows if index in (1, 5, 6, 7) else vrows)

    for h in range(heads):
        cols = head_cols(h)
        out[place(0), cols] = dot_tn(p1[h], win[1, :, cols]).astype(BF16)
        out[place(2), cols] = (dot_tn(ds1[h], win[0, :, cols]) * scale).astype(BF16)

    @pl.when(has_f)
    def _():
        ls_f.wait_recv()

    for p in range(pairs):
        factor, delta = joined(m_on[pl.ds(p, 1), :], [terms_of(es, p), terms_of(rl_f, p)])
        prob = e_on[p] * factor
        weights = prob.astype(BF16)
        dscore = (prob * (dp_on[p] - delta)).astype(BF16)
        s_video[0, :, pair_cols(p)] = (dot_nn(dscore[vrows:], qb[0, p, pl.ds(0, two), :]) * scale).astype(BF16)
        s_video[1, :, pair_cols(p)] = dot_nn(weights[vrows:], qb[1, p, pl.ds(0, two), :]).astype(BF16)
        kv_video[p].start()
        p2[p, :, pl.ds(0, two)] = weights[:vrows]
        ds2[p, :, pl.ds(0, two)] = dscore[:vrows]
        weights, dscore = weights.T, dscore.T
        for k in range(2):
            cols = head_cols(2 * p + k)
            rows = slice(k * arows, (k + 1) * arows)
            own_a[OUT, :, cols] = dot_nn(weights[rows], vkv[1, :, cols])
            own_a[DQ, :, cols] = dot_nn(dscore[rows], vkv[0, :, cols]) * scale

    for p in range(pairs):
        own_v[0, :, pair_cols(p)] = dot_nn(ds2[p], qb[0, p]) * scale
        own_v[1, :, pair_cols(p)] = dot_nn(p2[p], qb[1, p])

    for copy in near_in:
        copy.wait_send()

    @pl.when(has_f)
    def _():
        for copy in (*far_in[Q], *far_in[K], *far_in[V], *far_in[C], es_f):
            copy.wait_send()

    kv_near.wait_recv()
    for pair, copies, p in (
        ((DK, DV), kv_far, 0), ((DK, DV), kv_far, 1), ((OUT, DQ), oq_far, 0),
        ((OUT, DQ), oq_far, 1), ((OUT, DQ), oq_far, 2), ((DK, DV), kv_far, 2),
    ):
        @pl.when(has_f)
        def _(copy=copies[p]):
            copy.wait_recv()

        for t in pair:
            cols = pair_cols(p)
            total = own_a[t, :, cols] + r_far[t, :, cols].astype(F32)
            if t in (DK, DV):
                total += r_near[t, :, cols].astype(F32)
            out[place({OUT: 1, DQ: 5, DK: 6, DV: 7}[t]), cols] = total.astype(BF16)
    for p in range(pairs):
        kv_video[p].wait_recv()
        for t in range(2):
            cols = pair_cols(p)
            out[place(3 + t), cols] = (own_v[t, :, cols] + r_video[t, :, cols].astype(F32)).astype(BF16)

    for copy in (kv_near, *kv_video):
        copy.wait_send()

    @pl.when(has_f)
    def _():
        for copy in (*kv_far, *oq_far, ls_f):
            copy.wait_send()


def spread(sizes, joint, *refs):
    outs, sems = refs[: len(sizes)], refs[len(sizes)]
    start, copies = 0, []
    for index, size in enumerate(sizes):
        copies.append(pltpu.make_async_copy(joint.at[pl.ds(start, size)], outs[index], sems.at[index]))
        start += size
    for copy in copies:
        copy.start()
    for copy in copies:
        copy.wait()


def local(video_query, video_key, video_value, video_cot, audio_query, audio_key, audio_value, audio_cot, intersection):
    vrows, features = video_query.shape
    arows = audio_query.shape[0]
    heads = features // DH
    blocks = lax.axis_size("video")
    sizes = [vrows, arows, vrows, vrows, vrows, arows, arows, arows]
    dma = pltpu.SemaphoreType.DMA
    pairs = heads // 2
    two, three, wide = 2 * arows, 3 * arows, 2 * DH
    scratch = [
        pltpu.SMEM((2, blocks), jnp.int32),
        pltpu.VMEM((2, vrows, features), BF16),
        pltpu.VMEM((2, 2 * vrows, features), BF16),
        pltpu.VMEM((2, two, features), BF16),
        pltpu.VMEM((2, three, features), BF16),
        pltpu.VMEM((2, pairs, 2 * two, wide), BF16),
        *[pltpu.VMEM((pairs, 2 * vrows, two), F32)] * 2,
        *[pltpu.VMEM((pairs, vrows, two), F32)] * 2,
        *[pltpu.VMEM((heads, three, vrows), BF16)] * 2,
        *[pltpu.VMEM((pairs, vrows, 2 * two), BF16)] * 2,
        pltpu.VMEM((4, arows, features), F32),
        pltpu.VMEM((2, vrows, features), F32),
        *[pltpu.VMEM((2, arows, features), BF16)] * 2,
        *[pltpu.VMEM((2, vrows, features), BF16)] * 2,
        *[pltpu.VMEM((4, arows, features), BF16)] * 2,
        *[pltpu.VMEM((2, 4, two), F32)] * 4,
        *[pltpu.VMEM((4, two), F32)] * 2,
        pltpu.VMEM((three, vrows), F32),
        dma((9,)),
        *[dma((4,))] * 2,
        *[dma((4, pairs))] * 2,
        *[dma((2,))] * 2,
        *[dma((pairs,))] * 4,
        *[dma((1 + pairs,))] * 2,
    ]
    any_space = pl.BlockSpec(memory_space=pl.ANY)
    in_hbm = pl.BlockSpec(memory_space=pltpu.HBM)
    joint = pl.pallas_call(
        functools.partial(kernel, blocks, vrows, arows, heads),
        out_shape=pltpu.VMEM((sum(sizes), features), BF16),
        in_specs=[in_hbm] * 9,
        out_specs=pl.BlockSpec(memory_space=pltpu.VMEM),
        scratch_shapes=scratch,
        compiler_params=pltpu.CompilerParams(
            collective_id=0, has_side_effects=True, vmem_limit_bytes=24 * 1024 * 1024
        ),
        cost_estimate=pl.CostEstimate(
            flops=24 * heads * vrows * 3 * arows * DH, bytes_accessed=12 * (vrows + arows) * features, transcendentals=0
        ),
        name="cross_attention",
    )(*[pltpu.with_memory_space_constraint(x, pltpu.HBM) for x in (video_query, video_key, video_value, video_cot, audio_query, audio_key, audio_value, audio_cot, jnp.transpose(intersection))])
    joint = pltpu.with_memory_space_constraint(joint, pltpu.VMEM)
    return tuple(
        pl.pallas_call(
            functools.partial(spread, sizes),
            out_shape=[jax.ShapeDtypeStruct((size, features), BF16) for size in sizes],
            in_specs=[any_space],
            out_specs=[any_space] * len(sizes),
            scratch_shapes=[dma((len(sizes),))],
            name="spread",
        )(joint)
    )


def solution(mesh):
    rows = P(("clip", "video"), "audio")
    return jax.shard_map(
        local,
        mesh=mesh,
        in_specs=(rows,) * 8 + (P("clip", None),),
        out_specs=(rows,) * 8,
        check_vma=False,
    )
```

```python
import functools

import jax
import jax.numpy as jnp
from jax import lax
from jax.experimental import pallas as pl
from jax.experimental.pallas import tpu as pltpu
from jax.sharding import PartitionSpec as P

DH = 128
NEG = -1e30
ABSENT = -2e30
LOG2E = 1.4426950408889634
MESH = pl.DeviceIdType.MESH
F32 = jnp.float32
BF16 = jnp.bfloat16
Q, K, V, C = 0, 1, 2, 3
DK, DV, OUT, DQ = 0, 1, 2, 3
FIRST = ((K, 1), (V, 1), (Q, 0), (C, 0), (Q, 1), (C, 1))
LATER = ((Q, 2), (C, 2), (K, 2), (V, 2))


def dot_nt(a, b):
    return lax.dot_general(a, b, (((1,), (1,)), ((), ())), preferred_element_type=F32)


def dot_nn(a, b):
    return lax.dot_general(a, b, (((1,), (0,)), ((), ())), preferred_element_type=F32)


def dot_tn(a, b):
    return lax.dot_general(a, b, (((0,), (0,)), ((), ())), preferred_element_type=F32)


def joined(top_here, parts):
    top = functools.reduce(jnp.maximum, [p[0] for p in parts])
    shares = [jnp.exp2(p[0] - top) for p in parts]
    inverse = 1.0 / sum(shares)
    return jnp.exp2(top_here - top) * inverse, sum(w * p[1] for w, p in zip(shares, parts)) * inverse


def kernel(blocks, vrows, arows, heads, *refs):
    (vq, vk, vv, vc, aq, ak, av, ac, inter, out) = refs[:10]
    (spans, vqc, vkv, qc, win, qb, e_on, dp_on, e_far, dp_far, p1, ds1, p2, ds2, own_a, own_v,
     s_near, r_near, s_video, r_video, s_far, r_far, es, ls, re_f, rl_f, m_on, m_far, bias,
     load_sem, near_sem, far_sem, terms_sem, kv_sem, oq_sem, back_sem, sent) = refs[10:]
    scale = DH ** (-0.5)
    scale2 = scale * LOG2E
    two = 2 * arows
    three = 3 * arows
    pairs = heads // 2
    wide = 2 * DH

    b = lax.axis_index("video")
    odd = lax.rem(b, 2)
    n = b + 1 - 2 * odd
    f = b - 1 + 2 * odd
    has_f = (f >= 0) & (f < blocks)

    def here(index):
        return {"video": index}

    barrier = pltpu.get_barrier_semaphore()

    @pl.when(has_f)
    def _():
        pl.semaphore_signal(barrier, inc=1, device_id=here(f), device_id_type=MESH)

    pl.semaphore_signal(barrier, inc=1, device_id=here(n), device_id_type=MESH)

    span_load = pltpu.make_async_copy(inter, spans, load_sem.at[4])
    loads = [
        pltpu.make_async_copy(vk, vkv.at[0, pl.ds(0, vrows)], load_sem.at[0]),
        pltpu.make_async_copy(vv, vkv.at[1, pl.ds(0, vrows)], load_sem.at[0]),
        pltpu.make_async_copy(aq, qc.at[0, pl.ds(0, arows)], load_sem.at[1]),
        pltpu.make_async_copy(ac, qc.at[1, pl.ds(0, arows)], load_sem.at[1]),
        pltpu.make_async_copy(ak, win.at[0, pl.ds(0, arows)], load_sem.at[2]),
        pltpu.make_async_copy(av, win.at[1, pl.ds(0, arows)], load_sem.at[2]),
        pltpu.make_async_copy(vq, vqc.at[0], load_sem.at[3]),
        pltpu.make_async_copy(vc, vqc.at[1], load_sem.at[3]),
    ]
    for copy in (span_load, *loads):
        copy.start()

    def remote(src, dst, ssem, rsem, device):
        return pltpu.make_async_remote_copy(
            src_ref=src, dst_ref=dst, send_sem=ssem, recv_sem=rsem, device_id=here(device), device_id_type=MESH
        )

    def wait_for(ref, sem):
        pltpu.make_async_copy(ref, ref, sem).wait()

    def pair_cols(p):
        return pl.ds(p * wide, wide)

    def head_cols(h):
        return pl.ds(h * DH, DH)

    to_n, to_f = sent.at[0], sent.at[1]
    near_in = [
        remote(ref, dst, to_n, near_sem.at[t // 2], n)
        for t, (ref, dst) in enumerate((
            (vk, vkv.at[0, pl.ds(vrows, vrows)]),
            (vv, vkv.at[1, pl.ds(vrows, vrows)]),
            (ak, win.at[0, pl.ds(arows, arows)]),
            (av, win.at[1, pl.ds(arows, arows)]),
        ))
    ]
    far_in = [
        [remote(ref.at[:, pair_cols(p)], dst.at[:, pair_cols(p)], to_f, far_sem.at[kind, p], f) for p in range(pairs)]
        for ref, dst, kind in (
            (aq, qc.at[0, pl.ds(arows, arows)], 0),
            (ak, win.at[0, pl.ds(two, arows)], 1),
            (av, win.at[1, pl.ds(two, arows)], 1),
            (ac, qc.at[1, pl.ds(arows, arows)], 0),
        )
    ]
    es_f = remote(es, re_f, sent.at[2], terms_sem.at[0], f)
    ls_f = remote(ls, rl_f, sent.at[3], terms_sem.at[1], f)
    kv_far = [
        remote(s_far.at[pl.ds(0, 2), :, pair_cols(p)], r_far.at[pl.ds(0, 2), :, pair_cols(p)], to_f, kv_sem.at[p], f)
        for p in range(pairs)
    ]
    oq_far = [
        remote(s_far.at[pl.ds(2, 2), :, pair_cols(p)], r_far.at[pl.ds(2, 2), :, pair_cols(p)], to_f, oq_sem.at[p], f)
        for p in range(pairs)
    ]
    kv_near = remote(s_near, r_near, to_n, back_sem.at[pairs], n)
    kv_video = [
        remote(s_video.at[:, :, pair_cols(p)], r_video.at[:, :, pair_cols(p)], to_n, back_sem.at[p], n)
        for p in range(pairs)
    ]

    for p in range(pairs):
        for t in range(2):
            for half in range(2):
                rows = pl.ds(half * two, two)
                qb[t, p, rows, :] = jnp.zeros((two, wide), BF16)

    for ref in (es, ls, m_on, m_far):
        ref[...] = jnp.zeros_like(ref)

    pl.semaphore_wait(barrier, 1 + has_f.astype(jnp.int32))

    @pl.when(has_f)
    def _():
        far_in[K][0].start()
        far_in[V][0].start()

    for copy in near_in:
        copy.start()

    @pl.when(has_f)
    def _():
        for t, p in FIRST:
            far_in[t][p].start()

    span_load.wait()
    first, last = spans[0, b], spans[1, b]
    lane = lax.broadcasted_iota(jnp.int32, (1, two), 1)
    lane = jnp.where(lane < arows, lane, lane - arows)
    mask_far = (f * arows + lane >= first) & (f * arows + lane < last)
    mask_near = (b * arows + lane >= spans[0, n]) & (b * arows + lane < spans[1, n])
    bias_near = jnp.where(mask_near, 0.0, NEG)
    sub = lax.broadcasted_iota(jnp.int32, (three, vrows), 0)
    rows_sub = jnp.where(sub < arows, b * arows + sub,
                         jnp.where(sub < two, n * arows + sub - arows, f * arows + sub - two))
    bias[...] = jnp.where((rows_sub >= first) & (rows_sub < last), 0.0, NEG)

    @pl.when(jnp.logical_not(has_f))
    def _():
        for t in range(2):
            win[t, pl.ds(two, arows), :] = jnp.zeros((arows, heads * DH), BF16)
            qc[t, pl.ds(arows, arows), :] = jnp.zeros((arows, heads * DH), BF16)
        for t in range(4):
            r_far[t] = jnp.zeros((arows, heads * DH), BF16)
        for ref in (re_f, rl_f):
            ref[0] = jnp.full(ref.shape[1:], NEG, F32)
            ref[1] = jnp.zeros(ref.shape[1:], F32)

    wait_for(vkv.at[:, pl.ds(0, vrows)], load_sem.at[0])
    wait_for(qc.at[:, pl.ds(0, arows)], load_sem.at[1])
    wait_for(win.at[:, pl.ds(0, arows)], load_sem.at[2])
    wait_for(vqc, load_sem.at[3])

    def place_blocks(p, start):
        for t in range(2):
            for k in range(2):
                qb[t, p, pl.ds(2 * start + k * arows, arows), head_cols(k)] = (
                    qc[t, pl.ds(start, arows), head_cols(2 * p + k)]
                )

    for p in range(pairs):
        place_blocks(p, 0)

    wait_for(vkv.at[:, pl.ds(vrows, vrows)], near_sem.at[0])

    for p in range(pairs):
        s = dot_nt(vkv[0, :, pair_cols(p)], qb[0, p, pl.ds(0, two), :]) * scale2
        dp = dot_nt(vkv[1, :, pair_cols(p)], qb[1, p, pl.ds(0, two), :])
        s = jnp.concatenate([s[:vrows], s[vrows:] + bias_near], axis=0)
        top = jnp.max(s, axis=0, keepdims=True)
        e = jnp.exp2(s - top)
        e_on[p] = e
        dp_on[p] = dp
        total = jnp.sum(e, axis=0, keepdims=True)
        m_on[pl.ds(p, 1), :] = top
        es[0, pl.ds(p, 1), :] = top + jnp.log(total) * LOG2E
        es[1, pl.ds(p, 1), :] = jnp.sum(e * dp, axis=0, keepdims=True) / total

    @pl.when(has_f)
    def _():
        es_f.start()
        for t, p in LATER:
            far_in[t][p].start()

    wait_for(win.at[:, pl.ds(arows, arows)], near_sem.at[1])

    def stage_scores(p):
        @pl.when(has_f)
        def _():
            wait_for(win.at[:, pl.ds(two, arows), pair_cols(p)], far_sem.at[1, p])

        for h in (2 * p, 2 * p + 1):
            cols = head_cols(h)
            qv, cv = vqc[0, :, cols], vqc[1, :, cols]
            s = dot_nt(win[0, :, cols], qv) * scale2 + bias[...]
            dp = dot_nt(win[1, :, cols], cv)
            top = jnp.max(s, axis=0, keepdims=True)
            e = jnp.exp2(s - top)
            inverse = 1.0 / jnp.sum(e, axis=0, keepdims=True)
            prob = e * inverse
            delta = jnp.sum(prob * dp, axis=0, keepdims=True)
            weights = prob.astype(BF16)
            dscore = (prob * (dp - delta)).astype(BF16)
            p1[h] = weights
            ds1[h] = dscore
            s_far[DK, :, cols] = (dot_nn(dscore[two:], qv) * scale).astype(BF16)
            s_far[DV, :, cols] = dot_nn(weights[two:], cv).astype(BF16)

        @pl.when(has_f)
        def _():
            kv_far[p].start()

    def stage_terms(p):
        @pl.when(has_f)
        def _():
            wait_for(qc.at[:, pl.ds(arows, arows), pair_cols(p)], far_sem.at[0, p])

        place_blocks(p, arows)
        s = dot_nt(vkv[0, pl.ds(0, vrows), pair_cols(p)], qb[0, p, pl.ds(two, two), :]) * scale2
        dp = dot_nt(vkv[1, pl.ds(0, vrows), pair_cols(p)], qb[1, p, pl.ds(two, two), :])
        top = jnp.max(s, axis=0, keepdims=True)
        e = jnp.exp2(s - top)
        e_far[p] = e
        dp_far[p] = dp
        total = jnp.sum(e, axis=0, keepdims=True)
        m_far[pl.ds(p, 1), :] = jnp.where(mask_far, top, ABSENT)
        ls[0, pl.ds(p, 1), :] = jnp.where(mask_far, top + jnp.log(total) * LOG2E, NEG)
        ls[1, pl.ds(p, 1), :] = jnp.where(mask_far, jnp.sum(e * dp, axis=0, keepdims=True) / total, 0.0)

    def terms_of(ref, p):
        return [ref[0, pl.ds(p, 1), :], ref[1, pl.ds(p, 1), :]]

    def stage_far(p):
        factor, delta = joined(m_far[pl.ds(p, 1), :], [terms_of(ls, p), terms_of(re_f, p)])
        prob = e_far[p] * factor
        weights = prob.astype(BF16)
        dscore = (prob * (dp_far[p] - delta)).astype(BF16)
        p2[p, :, pl.ds(two, two)] = weights
        ds2[p, :, pl.ds(two, two)] = dscore
        weights, dscore = weights.T, dscore.T
        for k in range(2):
            cols = head_cols(2 * p + k)
            rows = slice(k * arows, (k + 1) * arows)
            s_far[OUT, :, cols] = dot_nn(weights[rows], vkv[1, pl.ds(0, vrows), cols]).astype(BF16)
            s_far[DQ, :, cols] = (dot_nn(dscore[rows], vkv[0, pl.ds(0, vrows), cols]) * scale).astype(BF16)

        @pl.when(has_f)
        def _():
            oq_far[p].start()

    stage_scores(0)
    stage_scores(1)
    stage_terms(0)

    @pl.when(has_f)
    def _():
        es_f.wait_recv()

    stage_far(0)
    stage_terms(1)
    stage_terms(2)

    @pl.when(has_f)
    def _():
        ls_f.start()

    stage_far(1)
    stage_far(2)
    stage_scores(2)

    for h in range(heads):
        cols = head_cols(h)
        dk = dot_nn(ds1[h, pl.ds(0, two), :], vqc[0, :, cols]) * scale
        dv = dot_nn(p1[h, pl.ds(0, two), :], vqc[1, :, cols])
        own_a[DK, :, cols] = dk[:arows]
        own_a[DV, :, cols] = dv[:arows]
        s_near[DK, :, cols] = dk[arows:].astype(BF16)
        s_near[DV, :, cols] = dv[arows:].astype(BF16)
    kv_near.start()

    def place(index):
        starts = [0, vrows, vrows + arows, 2 * vrows + arows, 3 * vrows + arows,
                  4 * vrows + arows, 4 * vrows + 2 * arows, 4 * vrows + 3 * arows]
        return pl.ds(starts[index], arows if index in (1, 5, 6, 7) else vrows)

    for h in range(heads):
        cols = head_cols(h)
        out[place(0), cols] = dot_tn(p1[h], win[1, :, cols]).astype(BF16)
        out[place(2), cols] = (dot_tn(ds1[h], win[0, :, cols]) * scale).astype(BF16)

    @pl.when(has_f)
    def _():
        ls_f.wait_recv()

    for p in range(pairs):
        factor, delta = joined(m_on[pl.ds(p, 1), :], [terms_of(es, p), terms_of(rl_f, p)])
        prob = e_on[p] * factor
        weights = prob.astype(BF16)
        dscore = (prob * (dp_on[p] - delta)).astype(BF16)
        s_video[0, :, pair_cols(p)] = (dot_nn(dscore[vrows:], qb[0, p, pl.ds(0, two), :]) * scale).astype(BF16)
        s_video[1, :, pair_cols(p)] = dot_nn(weights[vrows:], qb[1, p, pl.ds(0, two), :]).astype(BF16)
        kv_video[p].start()
        p2[p, :, pl.ds(0, two)] = weights[:vrows]
        ds2[p, :, pl.ds(0, two)] = dscore[:vrows]
        weights, dscore = weights.T, dscore.T
        for k in range(2):
            cols = head_cols(2 * p + k)
            rows = slice(k * arows, (k + 1) * arows)
            own_a[OUT, :, cols] = dot_nn(weights[rows], vkv[1, :, cols])
            own_a[DQ, :, cols] = dot_nn(dscore[rows], vkv[0, :, cols]) * scale

    for p in range(pairs):
        own_v[0, :, pair_cols(p)] = dot_nn(ds2[p], qb[0, p]) * scale
        own_v[1, :, pair_cols(p)] = dot_nn(p2[p], qb[1, p])

    for p in range(pairs):
        kv_video[p].wait_recv()
        for t in range(2):
            cols = pair_cols(p)
            out[place(3 + t), cols] = (own_v[t, :, cols] + r_video[t, :, cols].astype(F32)).astype(BF16)

    kv_near.wait_recv()
    for pair, copies, p in (
        ((DK, DV), kv_far, 0), ((DK, DV), kv_far, 1), ((OUT, DQ), oq_far, 0),
        ((OUT, DQ), oq_far, 1), ((OUT, DQ), oq_far, 2), ((DK, DV), kv_far, 2),
    ):
        @pl.when(has_f)
        def _(copy=copies[p]):
            copy.wait_recv()

        for t in pair:
            cols = pair_cols(p)
            total = own_a[t, :, cols] + r_far[t, :, cols].astype(F32)
            if t in (DK, DV):
                total += r_near[t, :, cols].astype(F32)
            out[place({OUT: 1, DQ: 5, DK: 6, DV: 7}[t]), cols] = total.astype(BF16)
    wait_for(out, to_n)

    @pl.when(has_f)
    def _():
        wait_for(out.at[pl.ds(0, 8 * arows)], to_f)
        es_f.wait_send()
        ls_f.wait_send()


def spread(sizes, joint, *refs):
    outs, sem = refs[: len(sizes)], refs[len(sizes)]
    start = 0
    for index, size in enumerate(sizes):
        pltpu.make_async_copy(joint.at[pl.ds(start, size)], outs[index], sem).start()
        start += size
    pltpu.make_async_copy(joint, joint, sem).wait()


def local(video_query, video_key, video_value, video_cot, audio_query, audio_key, audio_value, audio_cot, intersection):
    vrows, features = video_query.shape
    arows = audio_query.shape[0]
    heads = features // DH
    blocks = lax.axis_size("video")
    sizes = [vrows, arows, vrows, vrows, vrows, arows, arows, arows]
    dma = pltpu.SemaphoreType.DMA
    pairs = heads // 2
    two, three, wide = 2 * arows, 3 * arows, 2 * DH
    scratch = [
        pltpu.SMEM((2, blocks), jnp.int32),
        pltpu.VMEM((2, vrows, features), BF16),
        pltpu.VMEM((2, 2 * vrows, features), BF16),
        pltpu.VMEM((2, two, features), BF16),
        pltpu.VMEM((2, three, features), BF16),
        pltpu.VMEM((2, pairs, 2 * two, wide), BF16),
        *[pltpu.VMEM((pairs, 2 * vrows, two), F32)] * 2,
        *[pltpu.VMEM((pairs, vrows, two), F32)] * 2,
        *[pltpu.VMEM((heads, three, vrows), BF16)] * 2,
        *[pltpu.VMEM((pairs, vrows, 2 * two), BF16)] * 2,
        pltpu.VMEM((4, arows, features), F32),
        pltpu.VMEM((2, vrows, features), F32),
        *[pltpu.VMEM((2, arows, features), BF16)] * 2,
        *[pltpu.VMEM((2, vrows, features), BF16)] * 2,
        *[pltpu.VMEM((4, arows, features), BF16)] * 2,
        *[pltpu.VMEM((2, 4, two), F32)] * 4,
        *[pltpu.VMEM((4, two), F32)] * 2,
        pltpu.VMEM((three, vrows), F32),
        dma((5,)),
        dma((2,)),
        dma((2, pairs)),
        dma((2,)),
        *[dma((pairs,))] * 2,
        dma((1 + pairs,)),
        dma((4,)),
    ]
    any_space = pl.BlockSpec(memory_space=pl.ANY)
    in_hbm = pl.BlockSpec(memory_space=pltpu.HBM)
    joint = pl.pallas_call(
        functools.partial(kernel, blocks, vrows, arows, heads),
        out_shape=pltpu.VMEM((sum(sizes), features), BF16),
        in_specs=[in_hbm] * 9,
        out_specs=pl.BlockSpec(memory_space=pltpu.VMEM),
        scratch_shapes=scratch,
        compiler_params=pltpu.CompilerParams(
            collective_id=0, has_side_effects=True, vmem_limit_bytes=24 * 1024 * 1024
        ),
        cost_estimate=pl.CostEstimate(
            flops=24 * heads * vrows * 3 * arows * DH, bytes_accessed=12 * (vrows + arows) * features, transcendentals=0
        ),
        name="cross_attention",
    )(*[pltpu.with_memory_space_constraint(x, pltpu.HBM) for x in (video_query, video_key, video_value, video_cot, audio_query, audio_key, audio_value, audio_cot, jnp.transpose(intersection))])
    joint = pltpu.with_memory_space_constraint(joint, pltpu.VMEM)
    return tuple(
        pl.pallas_call(
            functools.partial(spread, sizes),
            out_shape=[jax.ShapeDtypeStruct((size, features), BF16) for size in sizes],
            in_specs=[any_space],
            out_specs=[any_space] * len(sizes),
            scratch_shapes=[dma],
            name="spread",
        )(joint)
    )


def solution(mesh):
    rows = P(("clip", "video"), "audio")
    return jax.shard_map(
        local,
        mesh=mesh,
        in_specs=(rows,) * 8 + (P("clip", None),),
        out_specs=(rows,) * 8,
        check_vma=False,
    )
```

```python
import functools

import jax
import jax.numpy as jnp
from jax import lax
from jax.experimental import pallas as pl
from jax.experimental.pallas import tpu as pltpu
from jax.sharding import PartitionSpec as P

DH = 128
NEG = -1e30
ABSENT = -2e30
LOG2E = 1.4426950408889634
MESH = pl.DeviceIdType.MESH
F32 = jnp.float32
BF16 = jnp.bfloat16
Q, K, V, C = 0, 1, 2, 3
DK, DV, OUT, DQ = 0, 1, 2, 3
KV_CHUNKS = ((0, 1), (1, 3), (3, 5), (5, 6))
QC, KV = 0, 1
FIRST = ((KV, 1), (QC, 0),)
LATER = ((QC, 1), (QC, 2), (KV, 2), (KV, 3),)


def dot_nt(a, b):
    return lax.dot_general(a, b, (((1,), (1,)), ((), ())), preferred_element_type=F32)


def dot_nn(a, b):
    return lax.dot_general(a, b, (((1,), (0,)), ((), ())), preferred_element_type=F32)


def dot_tn(a, b):
    return lax.dot_general(a, b, (((0,), (0,)), ((), ())), preferred_element_type=F32)


def joined(top_here, parts):
    top = functools.reduce(jnp.maximum, [p[0] for p in parts])
    shares = [jnp.exp2(p[0] - top) for p in parts]
    inverse = 1.0 / sum(shares)
    return jnp.exp2(top_here - top) * inverse, sum(w * p[1] for w, p in zip(shares, parts)) * inverse


def kernel(blocks, vrows, arows, heads, *refs):
    (vq, vk, vv, vc, aq, ak, av, ac, inter, out) = refs[:10]
    (spans, vqc, vkv, qc, win, qb, e_on, dp_on, e_far, dp_far, p1, ds1, p2, ds2, own_a, own_v,
     s_near, r_near, s_video, r_video, s_far, r_far, es, ls, re_f, rl_f, m_on, m_far, bias,
     load_sem, near_sem, qc_sem, far_sem, terms_sem, kv_sem, oq_sem, back_sem, sent) = refs[10:]
    scale = DH ** (-0.5)
    scale2 = scale * LOG2E
    two = 2 * arows
    three = 3 * arows
    pairs = heads // 2
    wide = 2 * DH

    b = lax.axis_index("video")
    odd = lax.rem(b, 2)
    n = b + 1 - 2 * odd
    f = b - 1 + 2 * odd
    has_f = (f >= 0) & (f < blocks)

    def here(index):
        return {"video": index}

    barrier = pltpu.get_barrier_semaphore()

    @pl.when(has_f)
    def _():
        pl.semaphore_signal(barrier, inc=1, device_id=here(f), device_id_type=MESH)

    pl.semaphore_signal(barrier, inc=1, device_id=here(n), device_id_type=MESH)

    span_load = pltpu.make_async_copy(inter, spans, load_sem.at[1])
    loads = [
        pltpu.make_async_copy(vk, vkv.at[0, pl.ds(0, vrows)], load_sem.at[0]),
        pltpu.make_async_copy(vv, vkv.at[1, pl.ds(0, vrows)], load_sem.at[0]),
        pltpu.make_async_copy(aq, qc.at[0, pl.ds(0, arows)], load_sem.at[0]),
        pltpu.make_async_copy(ac, qc.at[1, pl.ds(0, arows)], load_sem.at[0]),
        pltpu.make_async_copy(ak, win.at[0, pl.ds(0, arows)], load_sem.at[0]),
        pltpu.make_async_copy(av, win.at[1, pl.ds(0, arows)], load_sem.at[0]),
        pltpu.make_async_copy(vq, vqc.at[0], load_sem.at[0]),
        pltpu.make_async_copy(vc, vqc.at[1], load_sem.at[0]),
    ]
    for copy in (span_load, *loads):
        copy.start()

    def remote(src, dst, ssem, rsem, device):
        return pltpu.make_async_remote_copy(
            src_ref=src, dst_ref=dst, send_sem=ssem, recv_sem=rsem, device_id=here(device), device_id_type=MESH
        )

    def wait_for(ref, sem):
        pltpu.make_async_copy(ref, ref, sem).wait()

    def pair_cols(p):
        return pl.ds(p * wide, wide)

    def head_cols(h):
        return pl.ds(h * DH, DH)

    def chunk_cols(c):
        return pl.ds(KV_CHUNKS[c][0] * DH, (KV_CHUNKS[c][1] - KV_CHUNKS[c][0]) * DH)

    to_n, to_f = sent.at[0], sent.at[1]
    near_in = [
        remote(ref, dst, to_n, near_sem.at[t // 2], n)
        for t, (ref, dst) in enumerate((
            (vk, vkv.at[0, pl.ds(vrows, vrows)]),
            (vv, vkv.at[1, pl.ds(vrows, vrows)]),
            (ak, win.at[0, pl.ds(arows, arows)]),
            (av, win.at[1, pl.ds(arows, arows)]),
        ))
    ]
    far_qc = [
        [remote(ref.at[:, pair_cols(p)], qc.at[t, pl.ds(arows, arows), pair_cols(p)], to_f, qc_sem.at[p], f)
         for t, ref in enumerate((aq, ac))]
        for p in range(pairs)
    ]
    far_kv = [
        [remote(ref.at[:, chunk_cols(c)], win.at[t, pl.ds(two, arows), chunk_cols(c)], to_f, far_sem.at[c], f)
         for t, ref in enumerate((ak, av))]
        for c in range(len(KV_CHUNKS))
    ]
    es_f = remote(es, re_f, sent.at[2], terms_sem.at[0], f)
    ls_f = remote(ls, rl_f, sent.at[2], terms_sem.at[1], f)
    kv_far = [
        remote(s_far.at[pl.ds(0, 2), :, chunk_cols(c)], r_far.at[pl.ds(0, 2), :, chunk_cols(c)], to_f, kv_sem.at[c], f)
        for c in range(len(KV_CHUNKS))
    ]
    oq_far = [
        remote(s_far.at[pl.ds(2, 2), :, pair_cols(p)], r_far.at[pl.ds(2, 2), :, pair_cols(p)], to_f, oq_sem.at[p], f)
        for p in range(pairs)
    ]
    kv_near = remote(s_near, r_near, to_n, back_sem.at[0], n)
    kv_video = [
        remote(s_video.at[:, :, pair_cols(p)], r_video.at[:, :, pair_cols(p)], to_n, back_sem.at[1], n)
        for p in range(pairs)
    ]

    for p in range(pairs):
        for t in range(2):
            for half in range(2):
                rows = pl.ds(half * two, two)
                qb[t, p, rows, :] = jnp.zeros((two, wide), BF16)

    for ref in (es, ls, m_on, m_far):
        ref[...] = jnp.zeros_like(ref)

    pl.semaphore_wait(barrier, 1 + has_f.astype(jnp.int32))

    @pl.when(has_f)
    def _():
        for copy in far_kv[0]:
            copy.start()

    for copy in near_in:
        copy.start()

    @pl.when(has_f)
    def _():
        for kind, index in FIRST:
            for copy in (far_qc, far_kv)[kind][index]:
                copy.start()

    span_load.wait()
    first, last = spans[0, b], spans[1, b]
    lane = lax.broadcasted_iota(jnp.int32, (1, two), 1)
    lane = jnp.where(lane < arows, lane, lane - arows)
    mask_far = (f * arows + lane >= first) & (f * arows + lane < last)
    mask_near = (b * arows + lane >= spans[0, n]) & (b * arows + lane < spans[1, n])
    bias_near = jnp.where(mask_near, 0.0, NEG)
    sub = lax.broadcasted_iota(jnp.int32, (three, vrows), 0)
    rows_sub = jnp.where(sub < arows, b * arows + sub,
                         jnp.where(sub < two, n * arows + sub - arows, f * arows + sub - two))
    bias[...] = jnp.where((rows_sub >= first) & (rows_sub < last), 0.0, NEG)

    @pl.when(jnp.logical_not(has_f))
    def _():
        for t in range(2):
            win[t, pl.ds(two, arows), :] = jnp.zeros((arows, heads * DH), BF16)
            qc[t, pl.ds(arows, arows), :] = jnp.zeros((arows, heads * DH), BF16)
        for t in range(4):
            r_far[t] = jnp.zeros((arows, heads * DH), BF16)
        for ref in (re_f, rl_f):
            ref[0] = jnp.full(ref.shape[1:], NEG, F32)
            ref[1] = jnp.zeros(ref.shape[1:], F32)

    wait_for(out, load_sem.at[0])

    def place_blocks(p, start):
        for t in range(2):
            for k in range(2):
                qb[t, p, pl.ds(2 * start + k * arows, arows), head_cols(k)] = (
                    qc[t, pl.ds(start, arows), head_cols(2 * p + k)]
                )

    for p in range(pairs):
        place_blocks(p, 0)

    for p in range(pairs):
        e_on[p, pl.ds(0, vrows), :] = dot_nt(vkv[0, pl.ds(0, vrows), pair_cols(p)], qb[0, p, pl.ds(0, two), :]) * scale2
        dp_on[p, pl.ds(0, vrows), :] = dot_nt(vkv[1, pl.ds(0, vrows), pair_cols(p)], qb[1, p, pl.ds(0, two), :])

    wait_for(vkv.at[:, pl.ds(vrows, vrows)], near_sem.at[0])
    for p in range(pairs):
        near = pl.ds(vrows, vrows)
        s_own, dp_own = e_on[p, pl.ds(0, vrows), :], dp_on[p, pl.ds(0, vrows), :]
        s = dot_nt(vkv[0, near, pair_cols(p)], qb[0, p, pl.ds(0, two), :]) * scale2 + bias_near
        dp = dot_nt(vkv[1, near, pair_cols(p)], qb[1, p, pl.ds(0, two), :])
        top = jnp.maximum(jnp.max(s, axis=0, keepdims=True), jnp.max(s_own, axis=0, keepdims=True))
        e, e_own = jnp.exp2(s - top), jnp.exp2(s_own - top)
        e_on[p, pl.ds(0, vrows), :] = e_own
        e_on[p, near, :] = e
        dp_on[p, near, :] = dp
        total = jnp.sum(e + e_own, axis=0, keepdims=True)
        m_on[pl.ds(p, 1), :] = top
        es[0, pl.ds(p, 1), :] = top + jnp.log(total) * LOG2E
        es[1, pl.ds(p, 1), :] = jnp.sum(e * dp + e_own * dp_own, axis=0, keepdims=True) / total

    @pl.when(has_f)
    def _():
        es_f.start()
        for kind, index in LATER:
            for copy in (far_qc, far_kv)[kind][index]:
                copy.start()

    wait_for(win.at[:, pl.ds(arows, arows)], near_sem.at[1])

    def stage_scores(c):
        @pl.when(has_f)
        def _():
            wait_for(win.at[:, pl.ds(two, arows), chunk_cols(c)], far_sem.at[c])

        for h in range(*KV_CHUNKS[c]):
            cols = head_cols(h)
            qv, cv = vqc[0, :, cols], vqc[1, :, cols]
            s = dot_nt(win[0, :, cols], qv) * scale2 + bias[...]
            dp = dot_nt(win[1, :, cols], cv)
            top = jnp.max(s, axis=0, keepdims=True)
            e = jnp.exp2(s - top)
            inverse = 1.0 / jnp.sum(e, axis=0, keepdims=True)
            prob = e * inverse
            delta = jnp.sum(prob * dp, axis=0, keepdims=True)
            weights = prob.astype(BF16)
            dscore = (prob * (dp - delta)).astype(BF16)
            p1[h] = weights
            ds1[h] = dscore
            s_far[DK, :, cols] = (dot_nn(dscore[two:], qv) * scale).astype(BF16)
            s_far[DV, :, cols] = dot_nn(weights[two:], cv).astype(BF16)

        @pl.when(has_f)
        def _():
            kv_far[c].start()

    def stage_terms(p):
        @pl.when(has_f)
        def _():
            wait_for(qc.at[:, pl.ds(arows, arows), pair_cols(p)], qc_sem.at[p])

        place_blocks(p, arows)
        s = dot_nt(vkv[0, pl.ds(0, vrows), pair_cols(p)], qb[0, p, pl.ds(two, two), :]) * scale2
        dp = dot_nt(vkv[1, pl.ds(0, vrows), pair_cols(p)], qb[1, p, pl.ds(two, two), :])
        top = jnp.max(s, axis=0, keepdims=True)
        e = jnp.exp2(s - top)
        e_far[p] = e
        dp_far[p] = dp
        total = jnp.sum(e, axis=0, keepdims=True)
        m_far[pl.ds(p, 1), :] = jnp.where(mask_far, top, ABSENT)
        ls[0, pl.ds(p, 1), :] = jnp.where(mask_far, top + jnp.log(total) * LOG2E, NEG)
        ls[1, pl.ds(p, 1), :] = jnp.where(mask_far, jnp.sum(e * dp, axis=0, keepdims=True) / total, 0.0)

    def terms_of(ref, p):
        return [ref[0, pl.ds(p, 1), :], ref[1, pl.ds(p, 1), :]]

    def stage_far(p):
        factor, delta = joined(m_far[pl.ds(p, 1), :], [terms_of(ls, p), terms_of(re_f, p)])
        prob = e_far[p] * factor
        weights = prob.astype(BF16)
        dscore = (prob * (dp_far[p] - delta)).astype(BF16)
        p2[p, :, pl.ds(two, two)] = weights
        ds2[p, :, pl.ds(two, two)] = dscore
        weights, dscore = weights.T, dscore.T
        for k in range(2):
            cols = head_cols(2 * p + k)
            rows = slice(k * arows, (k + 1) * arows)
            s_far[OUT, :, cols] = dot_nn(weights[rows], vkv[1, pl.ds(0, vrows), cols]).astype(BF16)
            s_far[DQ, :, cols] = (dot_nn(dscore[rows], vkv[0, pl.ds(0, vrows), cols]) * scale).astype(BF16)

        @pl.when(has_f)
        def _():
            oq_far[p].start()

    stage_scores(0)
    stage_scores(1)
    stage_terms(0)

    @pl.when(has_f)
    def _():
        es_f.wait_recv()

    stage_far(0)
    stage_terms(1)
    stage_far(1)
    stage_terms(2)

    @pl.when(has_f)
    def _():
        ls_f.start()

    stage_far(2)
    stage_scores(2)
    stage_scores(3)

    for h in range(heads):
        cols = head_cols(h)
        dk = dot_nn(ds1[h, pl.ds(0, two), :], vqc[0, :, cols]) * scale
        dv = dot_nn(p1[h, pl.ds(0, two), :], vqc[1, :, cols])
        own_a[DK, :, cols] = dk[:arows]
        own_a[DV, :, cols] = dv[:arows]
        s_near[DK, :, cols] = dk[arows:].astype(BF16)
        s_near[DV, :, cols] = dv[arows:].astype(BF16)
    kv_near.start()

    def place(index):
        starts = [0, vrows, vrows + arows, 2 * vrows + arows, 3 * vrows + arows,
                  4 * vrows + arows, 4 * vrows + 2 * arows, 4 * vrows + 3 * arows]
        return pl.ds(starts[index], arows if index in (1, 5, 6, 7) else vrows)

    for h in range(heads):
        cols = head_cols(h)
        out[place(0), cols] = dot_tn(p1[h], win[1, :, cols]).astype(BF16)
        out[place(2), cols] = (dot_tn(ds1[h], win[0, :, cols]) * scale).astype(BF16)

    @pl.when(has_f)
    def _():
        ls_f.wait_recv()

    for p in range(pairs):
        factor, delta = joined(m_on[pl.ds(p, 1), :], [terms_of(es, p), terms_of(rl_f, p)])
        prob = e_on[p] * factor
        weights = prob.astype(BF16)
        dscore = (prob * (dp_on[p] - delta)).astype(BF16)
        s_video[0, :, pair_cols(p)] = (dot_nn(dscore[vrows:], qb[0, p, pl.ds(0, two), :]) * scale).astype(BF16)
        s_video[1, :, pair_cols(p)] = dot_nn(weights[vrows:], qb[1, p, pl.ds(0, two), :]).astype(BF16)
        kv_video[p].start()
        p2[p, :, pl.ds(0, two)] = weights[:vrows]
        ds2[p, :, pl.ds(0, two)] = dscore[:vrows]
        weights, dscore = weights.T, dscore.T
        for k in range(2):
            cols = head_cols(2 * p + k)
            rows = slice(k * arows, (k + 1) * arows)
            own_a[OUT, :, cols] = dot_nn(weights[rows], vkv[1, :, cols])
            own_a[DQ, :, cols] = dot_nn(dscore[rows], vkv[0, :, cols]) * scale

    for p in range(pairs):
        own_v[0, :, pair_cols(p)] = dot_nn(ds2[p], qb[0, p]) * scale
        own_v[1, :, pair_cols(p)] = dot_nn(p2[p], qb[1, p])

    wait_for(r_video, back_sem.at[1])
    for t in range(2):
        out[place(3 + t), :] = (own_v[t] + r_video[t].astype(F32)).astype(BF16)

    kv_near.wait_recv()
    for pair, copies, p in (
        ((DK, DV), kv_far, 0),
        ((DK, DV), kv_far, 1),
        ((OUT, DQ), oq_far, 0),
        ((OUT, DQ), oq_far, 1),
        ((OUT, DQ), oq_far, 2),
        ((DK, DV), kv_far, 2),
        ((DK, DV), kv_far, 3),
    ):
        @pl.when(has_f)
        def _(copy=copies[p]):
            copy.wait_recv()

        for t in pair:
            cols = chunk_cols(p) if copies is kv_far else pair_cols(p)
            total = own_a[t, :, cols] + r_far[t, :, cols].astype(F32)
            if t in (DK, DV):
                total += r_near[t, :, cols].astype(F32)
            out[place({OUT: 1, DQ: 5, DK: 6, DV: 7}[t]), cols] = total.astype(BF16)
    wait_for(out, to_n)

    @pl.when(has_f)
    def _():
        wait_for(out.at[pl.ds(0, 8 * arows)], to_f)
        wait_for(bias.at[pl.ds(0, 16)], sent.at[2])


def spread(sizes, joint, *refs):
    outs, sem = refs[: len(sizes)], refs[len(sizes)]
    start = 0
    for index, size in enumerate(sizes):
        pltpu.make_async_copy(joint.at[pl.ds(start, size)], outs[index], sem).start()
        start += size
    pltpu.make_async_copy(joint, joint, sem).wait()


def local(video_query, video_key, video_value, video_cot, audio_query, audio_key, audio_value, audio_cot, intersection):
    vrows, features = video_query.shape
    arows = audio_query.shape[0]
    heads = features // DH
    blocks = lax.axis_size("video")
    sizes = [vrows, arows, vrows, vrows, vrows, arows, arows, arows]
    dma = pltpu.SemaphoreType.DMA
    pairs = heads // 2
    two, three, wide = 2 * arows, 3 * arows, 2 * DH
    scratch = [
        pltpu.SMEM((2, blocks), jnp.int32),
        pltpu.VMEM((2, vrows, features), BF16),
        pltpu.VMEM((2, 2 * vrows, features), BF16),
        pltpu.VMEM((2, two, features), BF16),
        pltpu.VMEM((2, three, features), BF16),
        pltpu.VMEM((2, pairs, 2 * two, wide), BF16),
        *[pltpu.VMEM((pairs, 2 * vrows, two), F32)] * 2,
        *[pltpu.VMEM((pairs, vrows, two), F32)] * 2,
        *[pltpu.VMEM((heads, three, vrows), BF16)] * 2,
        *[pltpu.VMEM((pairs, vrows, 2 * two), BF16)] * 2,
        pltpu.VMEM((4, arows, features), F32),
        pltpu.VMEM((2, vrows, features), F32),
        *[pltpu.VMEM((2, arows, features), BF16)] * 2,
        *[pltpu.VMEM((2, vrows, features), BF16)] * 2,
        *[pltpu.VMEM((4, arows, features), BF16)] * 2,
        *[pltpu.VMEM((2, 4, two), F32)] * 4,
        *[pltpu.VMEM((4, two), F32)] * 2,
        pltpu.VMEM((three, vrows), F32),
        dma((2,)),
        dma((2,)),
        dma((pairs,)),
        dma((len(KV_CHUNKS),)),
        dma((2,)),
        dma((len(KV_CHUNKS),)),
        dma((pairs,)),
        dma((2,)),
        dma((3,)),
    ]
    any_space = pl.BlockSpec(memory_space=pl.ANY)
    in_hbm = pl.BlockSpec(memory_space=pltpu.HBM)
    joint = pl.pallas_call(
        functools.partial(kernel, blocks, vrows, arows, heads),
        out_shape=pltpu.VMEM((sum(sizes), features), BF16),
        in_specs=[in_hbm] * 9,
        out_specs=pl.BlockSpec(memory_space=pltpu.VMEM),
        scratch_shapes=scratch,
        compiler_params=pltpu.CompilerParams(
            collective_id=0, has_side_effects=True, vmem_limit_bytes=24 * 1024 * 1024
        ),
        cost_estimate=pl.CostEstimate(
            flops=24 * heads * vrows * 3 * arows * DH, bytes_accessed=12 * (vrows + arows) * features, transcendentals=0
        ),
        name="cross_attention",
    )(*[pltpu.with_memory_space_constraint(x, pltpu.HBM) for x in (video_query, video_key, video_value, video_cot, audio_query, audio_key, audio_value, audio_cot, jnp.transpose(intersection))])
    joint = pltpu.with_memory_space_constraint(joint, pltpu.VMEM)
    return tuple(
        pl.pallas_call(
            functools.partial(spread, sizes),
            out_shape=[jax.ShapeDtypeStruct((size, features), BF16) for size in sizes],
            in_specs=[any_space],
            out_specs=[any_space] * len(sizes),
            scratch_shapes=[dma],
            name="spread",
        )(joint)
    )


def solution(mesh):
    rows = P(("clip", "video"), "audio")
    return jax.shard_map(
        local,
        mesh=mesh,
        in_specs=(rows,) * 8 + (P("clip", None),),
        out_specs=(rows,) * 8,
        check_vma=False,
    )
```

```python
import functools

import jax
import jax.numpy as jnp
from jax import lax
from jax.experimental import pallas as pl
from jax.experimental.pallas import tpu as pltpu
from jax.sharding import PartitionSpec as P

DH = 128
NEG = -1e30
ABSENT = -2e30
LOG2E = 1.4426950408889634
MESH = pl.DeviceIdType.MESH
F32 = jnp.float32
BF16 = jnp.bfloat16
Q, K, V, C = 0, 1, 2, 3
DK, DV, OUT, DQ = 0, 1, 2, 3
KV_CHUNKS = ((0, 1), (1, 3), (3, 4), (4, 5), (5, 6))
QC, KV = 0, 1
FIRST = ((KV, 1), (KV, 2), (QC, 0))
LATER = ((QC, 1), (QC, 2), (KV, 3), (KV, 4))


def dot_nt(a, b):
    return lax.dot_general(a, b, (((1,), (1,)), ((), ())), preferred_element_type=F32)


def dot_nn(a, b):
    return lax.dot_general(a, b, (((1,), (0,)), ((), ())), preferred_element_type=F32)


def dot_tn(a, b):
    return lax.dot_general(a, b, (((0,), (0,)), ((), ())), preferred_element_type=F32)


def joined(top_here, parts):
    top = functools.reduce(jnp.maximum, [p[0] for p in parts])
    shares = [jnp.exp2(p[0] - top) for p in parts]
    inverse = 1.0 / sum(shares)
    return jnp.exp2(top_here - top) * inverse, sum(w * p[1] for w, p in zip(shares, parts)) * inverse


def kernel(blocks, vrows, arows, heads, *refs):
    (vq, vk, vv, vc, aq, ak, av, ac, inter, out) = refs[:10]
    (spans, vqc, vkv, qc, win, qb, e_on, dp_on, e_far, dp_far, p1, ds1, p2, ds2, own_a, own_v,
     s_near, r_near, s_video, r_video, s_far, r_far, es, ls, re_f, rl_f, m_on, m_far, bias,
     load_sem, near_sem, qc_sem, far_sem, terms_sem, kv_sem, oq_sem, back_sem, sent) = refs[10:]
    scale = DH ** (-0.5)
    scale2 = scale * LOG2E
    two = 2 * arows
    three = 3 * arows
    pairs = heads // 2
    wide = 2 * DH

    b = lax.axis_index("video")
    odd = lax.rem(b, 2)
    n = b + 1 - 2 * odd
    f = b - 1 + 2 * odd
    has_f = (f >= 0) & (f < blocks)

    def here(index):
        return {"video": index}

    barrier = pltpu.get_barrier_semaphore()

    @pl.when(has_f)
    def _():
        pl.semaphore_signal(barrier, inc=1, device_id=here(f), device_id_type=MESH)

    pl.semaphore_signal(barrier, inc=1, device_id=here(n), device_id_type=MESH)

    span_load = pltpu.make_async_copy(inter, spans, load_sem.at[1])
    loads = [
        pltpu.make_async_copy(vk, vkv.at[0, pl.ds(0, vrows)], load_sem.at[0]),
        pltpu.make_async_copy(vv, vkv.at[1, pl.ds(0, vrows)], load_sem.at[0]),
        pltpu.make_async_copy(aq, qc.at[0, pl.ds(0, arows)], load_sem.at[0]),
        pltpu.make_async_copy(ac, qc.at[1, pl.ds(0, arows)], load_sem.at[0]),
        pltpu.make_async_copy(ak, win.at[0, pl.ds(0, arows)], load_sem.at[0]),
        pltpu.make_async_copy(av, win.at[1, pl.ds(0, arows)], load_sem.at[0]),
        pltpu.make_async_copy(vq, vqc.at[0], load_sem.at[0]),
        pltpu.make_async_copy(vc, vqc.at[1], load_sem.at[0]),
    ]
    for copy in (span_load, *loads):
        copy.start()

    def remote(src, dst, ssem, rsem, device):
        return pltpu.make_async_remote_copy(
            src_ref=src, dst_ref=dst, send_sem=ssem, recv_sem=rsem, device_id=here(device), device_id_type=MESH
        )

    def wait_for(ref, sem):
        pltpu.make_async_copy(ref, ref, sem).wait()

    def pair_cols(p):
        return pl.ds(p * wide, wide)

    def head_cols(h):
        return pl.ds(h * DH, DH)

    def chunk_cols(c):
        return pl.ds(KV_CHUNKS[c][0] * DH, (KV_CHUNKS[c][1] - KV_CHUNKS[c][0]) * DH)

    to_n, to_f = sent.at[0], sent.at[1]
    near_in = [
        remote(ref, dst, to_n, near_sem.at[t // 2], n)
        for t, (ref, dst) in enumerate((
            (vk, vkv.at[0, pl.ds(vrows, vrows)]),
            (vv, vkv.at[1, pl.ds(vrows, vrows)]),
            (ak, win.at[0, pl.ds(arows, arows)]),
            (av, win.at[1, pl.ds(arows, arows)]),
        ))
    ]
    far_qc = [
        [remote(ref.at[:, pair_cols(p)], qc.at[t, pl.ds(arows, arows), pair_cols(p)], to_f, qc_sem.at[p], f)
         for t, ref in enumerate((aq, ac))]
        for p in range(pairs)
    ]
    far_kv = [
        [remote(ref.at[:, chunk_cols(c)], win.at[t, pl.ds(two, arows), chunk_cols(c)], to_f, far_sem.at[c], f)
         for t, ref in enumerate((ak, av))]
        for c in range(len(KV_CHUNKS))
    ]
    es_f = remote(es, re_f, sent.at[2], terms_sem.at[0], f)
    ls_f = remote(ls, rl_f, sent.at[2], terms_sem.at[1], f)
    kv_far = [
        remote(s_far.at[pl.ds(0, 2), :, chunk_cols(c)], r_far.at[pl.ds(0, 2), :, chunk_cols(c)], to_f, kv_sem.at[c], f)
        for c in range(len(KV_CHUNKS))
    ]
    oq_far = [
        remote(s_far.at[pl.ds(2, 2), :, pair_cols(p)], r_far.at[pl.ds(2, 2), :, pair_cols(p)], to_f, oq_sem.at[p], f)
        for p in range(pairs)
    ]
    kv_near = remote(s_near, r_near, to_n, back_sem.at[0], n)
    kv_video = [
        remote(s_video.at[:, :, pair_cols(p)], r_video.at[:, :, pair_cols(p)], to_n, back_sem.at[1], n)
        for p in range(pairs)
    ]

    for p in range(pairs):
        for t in range(2):
            for half in range(2):
                rows = pl.ds(half * two, two)
                qb[t, p, rows, :] = jnp.zeros((two, wide), BF16)

    for ref in (es, ls, m_on, m_far):
        ref[...] = jnp.zeros_like(ref)

    pl.semaphore_wait(barrier, 1 + has_f.astype(jnp.int32))

    @pl.when(has_f)
    def _():
        for copy in far_kv[0]:
            copy.start()

    for copy in near_in:
        copy.start()

    @pl.when(has_f)
    def _():
        for kind, index in FIRST:
            for copy in (far_qc, far_kv)[kind][index]:
                copy.start()

    span_load.wait()
    first, last = spans[0, b], spans[1, b]
    lane = lax.broadcasted_iota(jnp.int32, (1, two), 1)
    lane = jnp.where(lane < arows, lane, lane - arows)
    mask_far = (f * arows + lane >= first) & (f * arows + lane < last)
    mask_near = (b * arows + lane >= spans[0, n]) & (b * arows + lane < spans[1, n])
    bias_near = jnp.where(mask_near, 0.0, NEG)
    sub = lax.broadcasted_iota(jnp.int32, (three, vrows), 0)
    rows_sub = jnp.where(sub < arows, b * arows + sub,
                         jnp.where(sub < two, n * arows + sub - arows, f * arows + sub - two))
    bias[...] = jnp.where((rows_sub >= first) & (rows_sub < last), 0.0, NEG)

    @pl.when(jnp.logical_not(has_f))
    def _():
        for t in range(2):
            win[t, pl.ds(two, arows), :] = jnp.zeros((arows, heads * DH), BF16)
            qc[t, pl.ds(arows, arows), :] = jnp.zeros((arows, heads * DH), BF16)
        for t in range(4):
            r_far[t] = jnp.zeros((arows, heads * DH), BF16)
        for ref in (re_f, rl_f):
            ref[0] = jnp.full(ref.shape[1:], NEG, F32)
            ref[1] = jnp.zeros(ref.shape[1:], F32)

    wait_for(out, load_sem.at[0])

    def place_blocks(p, start):
        for t in range(2):
            for k in range(2):
                qb[t, p, pl.ds(2 * start + k * arows, arows), head_cols(k)] = (
                    qc[t, pl.ds(start, arows), head_cols(2 * p + k)]
                )

    for p in range(pairs):
        place_blocks(p, 0)

    for p in range(pairs):
        e_on[p, pl.ds(0, vrows), :] = dot_nt(vkv[0, pl.ds(0, vrows), pair_cols(p)], qb[0, p, pl.ds(0, two), :]) * scale2
        dp_on[p, pl.ds(0, vrows), :] = dot_nt(vkv[1, pl.ds(0, vrows), pair_cols(p)], qb[1, p, pl.ds(0, two), :])

    wait_for(vkv.at[:, pl.ds(vrows, vrows)], near_sem.at[0])
    for p in range(pairs):
        near = pl.ds(vrows, vrows)
        s_own, dp_own = e_on[p, pl.ds(0, vrows), :], dp_on[p, pl.ds(0, vrows), :]
        s = dot_nt(vkv[0, near, pair_cols(p)], qb[0, p, pl.ds(0, two), :]) * scale2 + bias_near
        dp = dot_nt(vkv[1, near, pair_cols(p)], qb[1, p, pl.ds(0, two), :])
        top = jnp.maximum(jnp.max(s, axis=0, keepdims=True), jnp.max(s_own, axis=0, keepdims=True))
        e, e_own = jnp.exp2(s - top), jnp.exp2(s_own - top)
        e_on[p, pl.ds(0, vrows), :] = e_own
        e_on[p, near, :] = e
        dp_on[p, near, :] = dp
        total = jnp.sum(e + e_own, axis=0, keepdims=True)
        m_on[pl.ds(p, 1), :] = top
        es[0, pl.ds(p, 1), :] = top + jnp.log(total) * LOG2E
        es[1, pl.ds(p, 1), :] = jnp.sum(e * dp + e_own * dp_own, axis=0, keepdims=True) / total

    @pl.when(has_f)
    def _():
        es_f.start()
        for kind, index in LATER:
            for copy in (far_qc, far_kv)[kind][index]:
                copy.start()

    wait_for(win.at[:, pl.ds(arows, arows)], near_sem.at[1])

    def stage_scores(c):
        @pl.when(has_f)
        def _():
            wait_for(win.at[:, pl.ds(two, arows), chunk_cols(c)], far_sem.at[c])

        for h in range(*KV_CHUNKS[c]):
            cols = head_cols(h)
            qv, cv = vqc[0, :, cols], vqc[1, :, cols]
            s = dot_nt(win[0, :, cols], qv) * scale2 + bias[...]
            dp = dot_nt(win[1, :, cols], cv)
            top = jnp.max(s, axis=0, keepdims=True)
            e = jnp.exp2(s - top)
            inverse = 1.0 / jnp.sum(e, axis=0, keepdims=True)
            prob = e * inverse
            delta = jnp.sum(prob * dp, axis=0, keepdims=True)
            weights = prob.astype(BF16)
            dscore = (prob * (dp - delta)).astype(BF16)
            p1[h] = weights
            ds1[h] = dscore
            s_far[DK, :, cols] = (dot_nn(dscore[two:], qv) * scale).astype(BF16)
            s_far[DV, :, cols] = dot_nn(weights[two:], cv).astype(BF16)

        @pl.when(has_f)
        def _():
            kv_far[c].start()

    def stage_terms(p):
        @pl.when(has_f)
        def _():
            wait_for(qc.at[:, pl.ds(arows, arows), pair_cols(p)], qc_sem.at[p])

        place_blocks(p, arows)
        s = dot_nt(vkv[0, pl.ds(0, vrows), pair_cols(p)], qb[0, p, pl.ds(two, two), :]) * scale2
        dp = dot_nt(vkv[1, pl.ds(0, vrows), pair_cols(p)], qb[1, p, pl.ds(two, two), :])
        top = jnp.max(s, axis=0, keepdims=True)
        e = jnp.exp2(s - top)
        e_far[p] = e
        dp_far[p] = dp
        total = jnp.sum(e, axis=0, keepdims=True)
        m_far[pl.ds(p, 1), :] = jnp.where(mask_far, top, ABSENT)
        ls[0, pl.ds(p, 1), :] = jnp.where(mask_far, top + jnp.log(total) * LOG2E, NEG)
        ls[1, pl.ds(p, 1), :] = jnp.where(mask_far, jnp.sum(e * dp, axis=0, keepdims=True) / total, 0.0)

    def terms_of(ref, p):
        return [ref[0, pl.ds(p, 1), :], ref[1, pl.ds(p, 1), :]]

    def stage_far(p):
        factor, delta = joined(m_far[pl.ds(p, 1), :], [terms_of(ls, p), terms_of(re_f, p)])
        prob = e_far[p] * factor
        weights = prob.astype(BF16)
        dscore = (prob * (dp_far[p] - delta)).astype(BF16)
        p2[p, :, pl.ds(two, two)] = weights
        ds2[p, :, pl.ds(two, two)] = dscore
        weights, dscore = weights.T, dscore.T
        for k in range(2):
            cols = head_cols(2 * p + k)
            rows = slice(k * arows, (k + 1) * arows)
            s_far[OUT, :, cols] = dot_nn(weights[rows], vkv[1, pl.ds(0, vrows), cols]).astype(BF16)
            s_far[DQ, :, cols] = (dot_nn(dscore[rows], vkv[0, pl.ds(0, vrows), cols]) * scale).astype(BF16)

        @pl.when(has_f)
        def _():
            oq_far[p].start()

    stage_scores(0)
    stage_scores(1)
    stage_scores(2)
    stage_terms(0)

    @pl.when(has_f)
    def _():
        es_f.wait_recv()

    stage_far(0)
    stage_terms(1)
    stage_far(1)
    stage_terms(2)

    @pl.when(has_f)
    def _():
        ls_f.start()

    stage_far(2)
    stage_scores(3)
    stage_scores(4)

    for h in range(heads):
        cols = head_cols(h)
        dk = dot_nn(ds1[h, pl.ds(0, two), :], vqc[0, :, cols]) * scale
        dv = dot_nn(p1[h, pl.ds(0, two), :], vqc[1, :, cols])
        own_a[DK, :, cols] = dk[:arows]
        own_a[DV, :, cols] = dv[:arows]
        s_near[DK, :, cols] = dk[arows:].astype(BF16)
        s_near[DV, :, cols] = dv[arows:].astype(BF16)
    kv_near.start()

    def place(index):
        starts = [0, vrows, vrows + arows, 2 * vrows + arows, 3 * vrows + arows,
                  4 * vrows + arows, 4 * vrows + 2 * arows, 4 * vrows + 3 * arows]
        return pl.ds(starts[index], arows if index in (1, 5, 6, 7) else vrows)

    for h in range(heads):
        cols = head_cols(h)
        out[place(0), cols] = dot_tn(p1[h], win[1, :, cols]).astype(BF16)
        out[place(2), cols] = (dot_tn(ds1[h], win[0, :, cols]) * scale).astype(BF16)

    @pl.when(has_f)
    def _():
        ls_f.wait_recv()

    for p in range(pairs):
        factor, delta = joined(m_on[pl.ds(p, 1), :], [terms_of(es, p), terms_of(rl_f, p)])
        prob = e_on[p] * factor
        weights = prob.astype(BF16)
        dscore = (prob * (dp_on[p] - delta)).astype(BF16)
        s_video[0, :, pair_cols(p)] = (dot_nn(dscore[vrows:], qb[0, p, pl.ds(0, two), :]) * scale).astype(BF16)
        s_video[1, :, pair_cols(p)] = dot_nn(weights[vrows:], qb[1, p, pl.ds(0, two), :]).astype(BF16)
        kv_video[p].start()
        p2[p, :, pl.ds(0, two)] = weights[:vrows]
        ds2[p, :, pl.ds(0, two)] = dscore[:vrows]
        weights, dscore = weights.T, dscore.T
        for k in range(2):
            cols = head_cols(2 * p + k)
            rows = slice(k * arows, (k + 1) * arows)
            own_a[OUT, :, cols] = dot_nn(weights[rows], vkv[1, :, cols])
            own_a[DQ, :, cols] = dot_nn(dscore[rows], vkv[0, :, cols]) * scale

    for p in range(pairs):
        own_v[0, :, pair_cols(p)] = dot_nn(ds2[p], qb[0, p]) * scale
        own_v[1, :, pair_cols(p)] = dot_nn(p2[p], qb[1, p])

    wait_for(r_video, back_sem.at[1])
    for t in range(2):
        out[place(3 + t), :] = (own_v[t] + r_video[t].astype(F32)).astype(BF16)

    kv_near.wait_recv()
    for pair, copies, p in (
        ((DK, DV), kv_far, 0),
        ((DK, DV), kv_far, 1),
        ((OUT, DQ), oq_far, 0),
        ((OUT, DQ), oq_far, 1),
        ((OUT, DQ), oq_far, 2),
        ((DK, DV), kv_far, 2),
        ((DK, DV), kv_far, 3),
        ((DK, DV), kv_far, 4),
    ):
        @pl.when(has_f)
        def _(copy=copies[p]):
            copy.wait_recv()

        for t in pair:
            cols = chunk_cols(p) if copies is kv_far else pair_cols(p)
            total = own_a[t, :, cols] + r_far[t, :, cols].astype(F32)
            if t in (DK, DV):
                total += r_near[t, :, cols].astype(F32)
            out[place({OUT: 1, DQ: 5, DK: 6, DV: 7}[t]), cols] = total.astype(BF16)
    wait_for(out, to_n)

    @pl.when(has_f)
    def _():
        wait_for(out.at[pl.ds(0, 8 * arows)], to_f)
        wait_for(bias.at[pl.ds(0, 16)], sent.at[2])


def spread(sizes, joint, *refs):
    outs, sem = refs[: len(sizes)], refs[len(sizes)]
    start = 0
    for index, size in enumerate(sizes):
        pltpu.make_async_copy(joint.at[pl.ds(start, size)], outs[index], sem).start()
        start += size
    pltpu.make_async_copy(joint, joint, sem).wait()


def local(video_query, video_key, video_value, video_cot, audio_query, audio_key, audio_value, audio_cot, intersection):
    vrows, features = video_query.shape
    arows = audio_query.shape[0]
    heads = features // DH
    blocks = lax.axis_size("video")
    sizes = [vrows, arows, vrows, vrows, vrows, arows, arows, arows]
    dma = pltpu.SemaphoreType.DMA
    pairs = heads // 2
    two, three, wide = 2 * arows, 3 * arows, 2 * DH
    scratch = [
        pltpu.SMEM((2, blocks), jnp.int32),
        pltpu.VMEM((2, vrows, features), BF16),
        pltpu.VMEM((2, 2 * vrows, features), BF16),
        pltpu.VMEM((2, two, features), BF16),
        pltpu.VMEM((2, three, features), BF16),
        pltpu.VMEM((2, pairs, 2 * two, wide), BF16),
        *[pltpu.VMEM((pairs, 2 * vrows, two), F32)] * 2,
        *[pltpu.VMEM((pairs, vrows, two), F32)] * 2,
        *[pltpu.VMEM((heads, three, vrows), BF16)] * 2,
        *[pltpu.VMEM((pairs, vrows, 2 * two), BF16)] * 2,
        pltpu.VMEM((4, arows, features), F32),
        pltpu.VMEM((2, vrows, features), F32),
        *[pltpu.VMEM((2, arows, features), BF16)] * 2,
        *[pltpu.VMEM((2, vrows, features), BF16)] * 2,
        *[pltpu.VMEM((4, arows, features), BF16)] * 2,
        *[pltpu.VMEM((2, 4, two), F32)] * 4,
        *[pltpu.VMEM((4, two), F32)] * 2,
        pltpu.VMEM((three, vrows), F32),
        dma((2,)),
        dma((2,)),
        dma((pairs,)),
        dma((len(KV_CHUNKS),)),
        dma((2,)),
        dma((len(KV_CHUNKS),)),
        dma((pairs,)),
        dma((2,)),
        dma((3,)),
    ]
    any_space = pl.BlockSpec(memory_space=pl.ANY)
    in_hbm = pl.BlockSpec(memory_space=pltpu.HBM)
    joint = pl.pallas_call(
        functools.partial(kernel, blocks, vrows, arows, heads),
        out_shape=pltpu.VMEM((sum(sizes), features), BF16),
        in_specs=[in_hbm] * 9,
        out_specs=pl.BlockSpec(memory_space=pltpu.VMEM),
        scratch_shapes=scratch,
        compiler_params=pltpu.CompilerParams(
            collective_id=0, has_side_effects=True, vmem_limit_bytes=24 * 1024 * 1024
        ),
        cost_estimate=pl.CostEstimate(
            flops=24 * heads * vrows * 3 * arows * DH, bytes_accessed=12 * (vrows + arows) * features, transcendentals=0
        ),
        name="cross_attention",
    )(*[pltpu.with_memory_space_constraint(x, pltpu.HBM) for x in (video_query, video_key, video_value, video_cot, audio_query, audio_key, audio_value, audio_cot, jnp.transpose(intersection))])
    joint = pltpu.with_memory_space_constraint(joint, pltpu.VMEM)
    return tuple(
        pl.pallas_call(
            functools.partial(spread, sizes),
            out_shape=[jax.ShapeDtypeStruct((size, features), BF16) for size in sizes],
            in_specs=[any_space],
            out_specs=[any_space] * len(sizes),
            scratch_shapes=[dma],
            name="spread",
        )(joint)
    )


def solution(mesh):
    rows = P(("clip", "video"), "audio")
    return jax.shard_map(
        local,
        mesh=mesh,
        in_specs=(rows,) * 8 + (P("clip", None),),
        out_specs=(rows,) * 8,
        check_vma=False,
    )
```
